128 devices in a mesh: set: 4 (over x), sub: 32 (over z, y, core).
Axes of the slice: x: 4, y: 4, z: 4, core: 2. Of those that a mesh axis runs over, the one named last changes fastest.
Arguments:
- jump_rhs: float32 [32, 1048576], P(None, ('set', 'sub')), may hold values from -21 to 21
- w_factor: bfloat16 [2048, 512, 512], P(('set', 'sub')), may hold values from -1 to 7
- s_factor: bfloat16 [2048, 512, 512], P(('set', 'sub')), may hold values from -1 to 7
- rigid_coarse_blocks: float32 [2048, 6, 512], P(('set', 'sub')), may hold values from -0.5 to 0.5
- coarse_factor: float32 [2048, 512], P('set'), may hold values from -1 to 5
- slot_of_row: int32 [1048576], P(('set', 'sub')), may hold values from 0 to 8191, as said below
- pair_counts: int32 [128, 32], P(('set', 'sub')), may hold values from 128 to 256, as said below
- corner_map: int32 [2048, 6], P(('set', 'sub')), may hold values from 0 to 511
Outputs:
- multipliers: float32 [32, 1048576], P(None, ('set', 'sub'))
- residual: float32 [32, 1048576], P(None, ('set', 'sub'))
The draws below stay inside these ranges and needn't reach their ends.
Inputs may be any that keep to these rules, and one draw needn't show every extreme that they name: `slot_of_row`: on each device the 8192 entries are a permutation of 0 to 8191; write a slot as j * 256 + i. On device d of a set (d its sub index) the row in slot j * 256 + i is paired with the row in slot d * 256 + i of device j of the same set when j != d, and with the row in slot d * 256 + (i xor 1) of device d itself when j == d. Slot j * 256 + i of device d is live exactly when i < pair_counts[d, j]. Within a set the table is symmetric in d and j, its diagonal is even, and some entry of every set equals 256.
All inputs are finite; a program needn't handle non-finite values.
Results may differ from the reference program's by a relative error of at most 0.0056.
Values sent between devices are 32-bit elements; how exact they have to be, the bound alone decides.
A program may use at most 192 MiB of HBM per device.

```python
import math
import jax
import jax.numpy as jnp
from jax import lax

L = 32
RM = 512
NC = 6
SD = 16
ITERS = 2
SETS = 4
PEERS = 32
DEVS = 128
RD = 8192
CAP = 256
SUBS = 2048
ROWS = 1048576
NCO = 512


def dominant(key, count, size, low, high, spread):
    key_diag, key_off = jax.random.split(key)
    diag = jnp.exp(jax.random.uniform(key_diag, (count, size), jnp.float32, math.log(low), math.log(high)))
    off = jnp.clip(jax.random.normal(key_off, (count, size, size), jnp.float32), -4.0, 4.0) * (spread / math.sqrt(size))
    ident = (jnp.arange(size)[:, None] == jnp.arange(size)[None, :]).astype(jnp.float32)
    return off * (1.0 - ident)[None] + ident[None] * diag[:, :, None]


def draw_jump_rhs(key, part):
    key = jax.random.fold_in(key, 11)
    frac = jnp.arange(ROWS, dtype=jnp.float32) / ROWS
    base = jnp.clip(jax.random.normal(key, (L, ROWS), jnp.float32), -4.0, 4.0)
    scale = 1.0 + 2.0 * frac
    return (base * scale[None, :]).astype(jnp.float32)


def draw_w_factor(key, part):
    key = jax.random.fold_in(key, 21)
    values = dominant(key, SUBS, RM, 1.0, 3.0, 1.0)
    return values.astype(jnp.bfloat16)


def draw_s_factor(key, part):
    key = jax.random.fold_in(key, 22)
    values = dominant(key, SUBS, RM, 1.0, 3.0, 1.0)
    return values.astype(jnp.bfloat16)


def draw_coarse_factor(key, part):
    key = jax.random.fold_in(key, 23)
    values = dominant(key, SETS, NCO, 1.0, 2.0, 0.5)
    return values.reshape(SETS * NCO, NCO).astype(jnp.float32)


def draw_slot_of_row(key, part):
    key = jax.random.fold_in(key, 31)
    keys = jax.random.split(key, DEVS)

    def one_perm(single):
        return jax.random.permutation(single, RD)
    perms = jax.vmap(one_perm)(keys)
    return perms.reshape(ROWS).astype(jnp.int32)


def draw_pair_counts(key, part):
    key = jax.random.fold_in(key, 32)
    key_table, key_diag = jax.random.split(key)
    table = jax.random.randint(key_table, (SETS, PEERS, PEERS), CAP // 2, CAP + 1)
    index = jnp.arange(PEERS)
    upper = index[:, None] <= index[None, :]
    table = jnp.where(upper[None], table, jnp.swapaxes(table, 1, 2))
    diag_vals = CAP - 2 * jax.random.randint(key_diag, (SETS, PEERS), 0, CAP // 4 + 1)
    ident = index[:, None] == index[None, :]
    table = jnp.where(ident[None], diag_vals[:, :, None], table)
    corner = (index[:, None] == 0) & (index[None, :] == 1) | (index[:, None] == 1) & (index[None, :] == 0)
    table = jnp.where(corner[None], CAP, table)
    return table.reshape(DEVS, PEERS).astype(jnp.int32)


def with_ends(values, key, smallest, largest):
    shape = values.shape
    spot = [jax.random.randint(jax.random.fold_in(key, axis), (), 0, shape[axis]) for axis in range(len(shape))]
    values = values.at[tuple(spot)].set(smallest)
    longest = shape.index(max(shape))
    spot[longest] = (spot[longest] + 1) % shape[longest]
    return values.at[tuple(spot)].set(largest)


def levels(stream_key, dims, cuts, smallest, top_value):
    level = 1.0
    for axis_at, blocks in cuts:
        draws = jax.random.uniform(jax.random.fold_in(jax.random.fold_in(stream_key, 6), axis_at), (blocks,), jnp.float32, smallest / len(cuts), top_value / len(cuts))
        level = level * jnp.repeat(jnp.exp(draws), dims[axis_at] // blocks).reshape((-1,) + (1,) * (len(dims) - 1 - axis_at))
    return level


def centred(stream_key, shape, scale, bound, cuts=(), kind=jnp.bfloat16):
    drawn = scale * jax.random.normal(stream_key, shape, jnp.float32)
    if cuts:
        drawn = drawn * levels(stream_key, shape, cuts, -0.22, 0.18)
    return jnp.clip(drawn, -bound, bound).astype(kind)


def setup_inputs(seed: int = 0) -> dict:
    streams_of = jax.random.split(jax.random.key(seed), 9)
    jump_rhs = draw_jump_rhs(jax.random.fold_in(streams_of[8], 71), 0)
    w_factor = draw_w_factor(jax.random.fold_in(streams_of[8], 71), 0)
    s_factor = draw_s_factor(jax.random.fold_in(streams_of[8], 71), 0)
    rigid_coarse_blocks = centred(streams_of[3], (SUBS, NC, RM), (RM // 4) ** -0.5, 0.5, ((0, 128),), jnp.float32)
    coarse_factor = draw_coarse_factor(jax.random.fold_in(streams_of[8], 71), 0)
    slot_of_row = draw_slot_of_row(jax.random.fold_in(streams_of[8], 71), 0)
    pair_counts = draw_pair_counts(jax.random.fold_in(streams_of[8], 71), 0)
    corner_map = with_ends(jax.random.randint(streams_of[7], (SUBS, NC), 0, NCO), jax.random.fold_in(streams_of[7], 1), 0, NCO - 1).astype(jnp.int32)
    return {"jump_rhs": jump_rhs, "w_factor": w_factor, "s_factor": s_factor, "rigid_coarse_blocks": rigid_coarse_blocks, "coarse_factor": coarse_factor, "slot_of_row": slot_of_row, "pair_counts": pair_counts, "corner_map": corner_map}


highest_accuracy = lax.Precision.HIGHEST


def live_rows(slot_of_row, pair_counts):
    slots = slot_of_row.reshape(DEVS, RD)
    flat = jnp.arange(RD, dtype=jnp.int32)
    live_slot = (flat % CAP)[None, :] < pair_counts[:, flat // CAP]
    live = jnp.take_along_axis(live_slot, slots, axis=1)
    return live.reshape(ROWS).astype(jnp.float32)


def pair_values(vector, slot_of_row):
    slots = slot_of_row.reshape(DEVS, RD)
    row_of_slot = jnp.argsort(slots, axis=1).astype(jnp.int32)
    flat = jnp.arange(RD, dtype=jnp.int32)
    my_index = jnp.arange(DEVS, dtype=jnp.int32) % PEERS
    source = jnp.where((flat // CAP)[None, :] == my_index[:, None], (flat ^ 1)[None, :], flat[None, :])
    send_rows = jnp.take_along_axis(row_of_slot, source.astype(jnp.int32), axis=1)
    reshaped_rows = vector.reshape(L, DEVS, RD)
    packed = jnp.take_along_axis(reshaped_rows, jnp.broadcast_to(send_rows[None], reshaped_rows.shape), axis=2)
    packed = packed.reshape(L, SETS, PEERS, PEERS, CAP)
    received = jnp.swapaxes(packed, 2, 3).reshape(L, DEVS, RD)
    paired = jnp.take_along_axis(received, jnp.broadcast_to(slots[None], reshaped_rows.shape), axis=2)
    return paired.reshape(L, ROWS)


def apply_factor(vector, cholesky_factor):
    vec_dev = jnp.transpose(vector.reshape(L, DEVS, SD, RM), (1, 0, 2, 3))
    fac_dev = cholesky_factor.reshape(DEVS, SD, RM, RM)

    def one_device(pair):
        vec_part, fac_part = pair
        rounded_values = lax.optimization_barrier(vec_part.astype(jnp.bfloat16)).astype(jnp.float32)
        widened_values = fac_part.astype(jnp.float32)
        half_product = jnp.einsum("muq,uqg->mug", rounded_values, widened_values, precision=highest_accuracy)
        half_product = lax.optimization_barrier(half_product.astype(jnp.bfloat16)).astype(jnp.float32)
        return jnp.einsum("gzf,zbf->gzb", half_product, widened_values, precision=highest_accuracy)

    final_output = lax.map(one_device, (vec_dev, fac_dev))
    return jnp.transpose(final_output, (1, 0, 2, 3)).reshape(L, ROWS)


def coarse_term(direction, rigid_coarse_blocks, coarse_factor, corner_map):
    reshaped_rows = direction.reshape(L, SUBS, RM)
    local_coarse_part = jnp.einsum("ejn,jbn->ejb", reshaped_rows, rigid_coarse_blocks, precision=highest_accuracy)
    grouped = local_coarse_part.reshape(L, SETS, PEERS * SD * NC)
    corners = corner_map.reshape(SETS, PEERS * SD * NC)
    onehot = (corners[:, :, None] == jnp.arange(NCO, dtype=jnp.int32)[None, None, :]).astype(jnp.float32)
    coarse_in = jnp.einsum("lxk,xkc->xlc", grouped, onehot, precision=highest_accuracy)
    lower = coarse_factor.reshape(SETS, NCO, NCO)
    middle = jnp.einsum("xlc,xcd->xld", coarse_in, lower, precision=highest_accuracy)
    coarse_sol = jnp.einsum("xld,xcd->xlc", middle, lower, precision=highest_accuracy)
    coarse_back_solve = jnp.einsum("xlc,xkc->lxk", coarse_sol, onehot, precision=highest_accuracy).reshape(L, SUBS, NC)
    back_solve = jnp.einsum("tbv,bvu->tbu", coarse_back_solve, rigid_coarse_blocks, precision=highest_accuracy)
    return back_solve.reshape(L, ROWS)


def reference(jump_rhs, w_factor, s_factor, rigid_coarse_blocks, coarse_factor, slot_of_row, pair_counts, corner_map):
    live = live_rows(slot_of_row, pair_counts)

    def pairing(vector):
        return live * (vector + pair_values(vector, slot_of_row))

    def precondition(vector):
        return pairing(apply_factor(pairing(vector), s_factor))

    residual = live * jump_rhs
    multipliers = jnp.zeros((L, ROWS), jnp.float32)
    precond = precondition(residual)
    energy = jnp.sum(residual * precond, axis=1)
    direction = precond
    for turn_index in range(ITERS):
        flexed = apply_factor(pairing(direction), w_factor)
        image = pairing(flexed) + live * coarse_term(direction, rigid_coarse_blocks, coarse_factor, corner_map)
        step_alpha = energy / jnp.sum(direction * image, axis=1)
        multipliers = multipliers + step_alpha[:, None] * direction
        residual = residual - step_alpha[:, None] * image
        if turn_index + 1 < ITERS:
            precond = precondition(residual)
            new_energy = jnp.sum(residual * precond, axis=1)
            direction = precond + (new_energy / energy)[:, None] * direction
            energy = new_energy
    return multipliers, residual
```

```python
import jax
import jax.numpy as jnp
from jax import lax
from jax.experimental import pallas as pl
from jax.experimental.pallas import tpu as pltpu
from jax.sharding import PartitionSpec as P

f32 = jnp.float32
bf16 = jnp.bfloat16
MESH = pl.DeviceIdType.MESH
HI = lax.Precision.HIGHEST

L = 32
PEERS = 32
SETS = 4
CAP = 256
RD = 8192
SD = 16
RM = 512
NC = 8
NK = SD * NC
NCO = 512
GROUP = 8
GROUPS = PEERS // GROUP

NT = (((1,), (1,)), ((), ()))


def dot(a, b):
    return jnp.dot(a, b, preferred_element_type=f32)


def dot_nt(a, b):
    return lax.dot_general(a, b, NT, preferred_element_type=f32)


def at(i, n):
    return pl.ds(pl.multiple_of(i * n, n), n)


def loop(n, f):
    def step(i, carry):
        f(i)
        return carry

    lax.fori_loop(0, n, step, 0)


def split(x):
    high = x.astype(bf16)
    return high, (x - high.astype(f32)).astype(bf16)


def kernel(
    jump, w_hbm, s_hbm, blocks, factor, slot, counts, corner,
    mult, resid,
    W, V, B, BT, Xm, live, jr, f, p, d, kd, pk,
    send, recv, csend, crecv, cpad, crow, Cbd, Ce, OHT,
    gsend, grecv, gall, back, pks, psend, precv, qsend, qrecv, acc,
    wsem, ssem, rsem, qssem, qrsem,
):
    st = lax.axis_index("set")
    me = lax.axis_index("sub")
    mg = me // GROUP

    copy_v = pltpu.make_async_copy(s_hbm, V, wsem.at[0])
    copy_w = pltpu.make_async_copy(w_hbm, W, wsem.at[1])
    copy_v.start()
    copy_w.start()

    barrier = pltpu.get_barrier_semaphore()

    def greet(k):
        pl.semaphore_signal(
            barrier, inc=1, device_id=(st, lax.rem(me + 1 + k, PEERS)), device_id_type=MESH
        )

    def greet_set(k):
        pl.semaphore_signal(
            barrier, inc=1, device_id=(lax.rem(st + 1 + k, SETS), me), device_id_type=MESH
        )

    loop(PEERS - 1, greet)
    loop(SETS - 1, greet_set)

    def remote(e, src, dst, q):
        return pltpu.make_async_remote_copy(
            src_ref=src, dst_ref=dst, send_sem=ssem.at[e, q], recv_sem=rsem.at[e, me],
            device_id=(st, q), device_id_type=MESH,
        )

    def arrival(e, dst, q):
        return pltpu.make_async_remote_copy(
            src_ref=dst, dst_ref=dst, send_sem=ssem.at[e, q], recv_sem=rsem.at[e, q],
            device_id=(st, q), device_id_type=MESH,
        )

    def others(f):
        def one(k):
            f(lax.rem(me + 1 + k, PEERS))

        loop(PEERS - 1, one)

    def group_others(g, f):
        def one(k):
            q = g * GROUP + lax.rem(me + k, GROUP)

            @pl.when(q != me)
            def _():
                f(q)

        loop(GROUP, one)

    def swap_pairs(x):
        lane = lax.broadcasted_iota(jnp.int32, x.shape, 1)
        n = x.shape[1]
        return jnp.where(lane % 2 == 0, pltpu.roll(x, n - 1, 1), pltpu.roll(x, 1, 1))

    def slots_and_send(e, x):
        def one(i):
            g = lax.rem(mg + i, GROUPS)
            for c in range(RD // CAP):
                cols = slice(c * CAP, (c + 1) * CAP)
                a = jnp.broadcast_to(slot[0:1, cols] // CAP - g * GROUP, (L, CAP))
                v = x[:, cols]
                Xm[:, cols] = jnp.concatenate(
                    [jnp.where(a == k, v, 0.0).astype(bf16) for k in range(GROUP)], axis=0
                )
            send[pl.ds(g * GROUP, GROUP)] = dot(Xm[...], BT[...]).reshape(GROUP, L, CAP)
            group_others(g, lambda q: remote(e, send.at[q], recv.at[e % 2, me], q).start())

        loop(GROUPS, one)
        recv[e % 2, me] = swap_pairs(send[me])

    def sent(e):
        others(lambda q: remote(e, send.at[q], recv.at[e % 2, me], q).wait_send())

    def rows_of_group(g, blocks16, out, first):
        for c in range(RD // CAP):
            cols = slice(c * CAP, (c + 1) * CAP)
            a = jnp.broadcast_to(slot[0:1, cols] // CAP - g * GROUP, (L, CAP))
            u = dot(blocks16, B[:, cols])
            res = out[:, cols]
            for k in range(GROUP):
                res = jnp.where(a == k, u[k * L : (k + 1) * L], res)
            out[:, cols] = res

    def receive_rows(e, out):
        out[...] = jnp.zeros_like(out)

        def one(i):
            g = lax.rem(mg + GROUPS - i, GROUPS)
            group_others(g, lambda q: arrival(e, recv.at[e % 2, q], q).wait_recv())
            blk = recv[e % 2, pl.ds(g * GROUP, GROUP)].reshape(GROUP * L, CAP).astype(bf16)
            rows_of_group(g, blk, out, False)

        loop(GROUPS, one)
        sent(e)

    def apply(x, F, scale):
        acc[...] = jnp.zeros_like(acc)

        def one(i):
            for k in range(4):
                s = i * 4 + k
                cols = at(s, RM)
                v = x[:, cols] * scale
                m = F[s]
                t = dot(v.astype(bf16), m).astype(bf16)
                out = dot_nt(t, m)
                f[:, cols] = out
                prod = v * out
                acc[...] += sum(prod[:, n * 128 : (n + 1) * 128] for n in range(RM // 128))

        loop(SD // 4, one)

    def lanes_to_row(x):
        x = jnp.concatenate([x, jnp.zeros((128 - L, 128), f32)], axis=0)
        return jnp.broadcast_to(jnp.sum(x.T, axis=0, keepdims=True), (8, 128))

    def row_to_column(x):
        return jnp.broadcast_to(x[0:1], (128, 128)).T[0:L]

    def sum_start(e):
        psend[e] = lanes_to_row(acc[...])
        precv[e, me] = psend[e]
        others(lambda q: remote(8 + e, psend.at[e], precv.at[e, me], q).start())

    def across(e, q):
        return pltpu.make_async_remote_copy(
            src_ref=qsend.at[e], dst_ref=qrecv.at[e, st], send_sem=qssem.at[e, q],
            recv_sem=qrsem.at[e, st], device_id=(q, me), device_id_type=MESH,
        )

    def across_arrival(e, q):
        return pltpu.make_async_remote_copy(
            src_ref=qsend.at[e], dst_ref=qrecv.at[e, q], send_sem=qssem.at[e, q],
            recv_sem=qrsem.at[e, q], device_id=(q, me), device_id_type=MESH,
        )

    def other_sets(f):
        loop(SETS - 1, lambda k: f(lax.rem(st + 1 + k, SETS)))

    def sum_middle(e, extra):
        others(lambda q: arrival(8 + e, precv.at[e, q], q).wait_recv())
        others(lambda q: remote(8 + e, psend.at[e], precv.at[e, me], q).wait_send())
        total = jnp.sum(precv[e], axis=0)
        if extra is not None:
            total = total + extra
        qsend[e] = total
        qrecv[e, st] = total
        other_sets(lambda q: across(e, q).start())

    def sum_end(e):
        other_sets(lambda q: across_arrival(e, q).wait_recv())
        other_sets(lambda q: across(e, q).wait_send())
        return row_to_column(jnp.sum(qrecv[e], axis=0))

    def coarse_start(e):
        gsend[e] = dot_nt(d[...].astype(bf16), Cbd[...])
        grecv[e, me] = gsend[e]
        others(lambda q: remote(6 + e, gsend.at[e], grecv.at[e, me], q).start())

    def coarse_solve(e):
        others(lambda q: arrival(6 + e, grecv.at[e, q], q).wait_recv())
        others(lambda q: remote(6 + e, gsend.at[e], grecv.at[e, me], q).wait_send())
        for j in range(PEERS):
            high, low = split(grecv[e, j])
            gall[:, j * NK : (j + 1) * NK] = jnp.concatenate([high, low], axis=0)
        both = dot_nt(gall[...], OHT[...])
        middle = jnp.dot(both[:L] + both[L:], factor[...], precision=HI, preferred_element_type=f32)
        sol = lax.dot_general(
            middle, factor[...], NT, precision=HI, preferred_element_type=f32
        )
        both = dot(jnp.concatenate(split(sol), axis=0), OHT[...])
        back[...] = both[:L] + both[L:]
        kd[...] = dot(back[:, at(me, NK)].astype(bf16), Cbd[...])
        square = middle * middle
        return lanes_to_row(sum(square[:, n * 128 : (n + 1) * 128] for n in range(NCO // 128)))

    def partners_coarse():
        def one(j):
            pks[pl.ds(pl.multiple_of(j * L, L), L), :] = dot(
                back[:, at(j, NK)].astype(bf16), Ce[j]
            ).astype(bf16)

        loop(PEERS, one)
        pk[...] = jnp.zeros_like(pk)
        loop(
            GROUPS,
            lambda g: rows_of_group(g, pks[at(g, GROUP * L), :], pk, False),
        )

    def onehot(c):
        cols = at(c, CAP)
        hit = lax.broadcasted_iota(jnp.int32, (CAP, CAP), 0) == slot[0:1, cols] % CAP
        m = jnp.where(hit, 1.0, 0.0)
        B[:, cols] = m.astype(bf16)
        BT[cols, :] = m.T.astype(bf16)

    loop(RD // CAP, onehot)

    def live_rows(c):
        cols = at(c, RM)
        s = slot[0:1, cols]
        a = s // CAP
        n = jnp.zeros_like(s)
        for k in range(PEERS):
            n = jnp.where(a == k, counts[0, k], n)
        on = jnp.where(s % CAP < n, 1.0, 0.0)
        live[:, cols] = jnp.broadcast_to(on, (8, RM))
        resid[:, cols] = on * jump[:, cols]

    loop(RD // RM, live_rows)

    cpad[...] = jnp.zeros_like(cpad)
    for s in range(SD):
        cpad[s, 0:6, :] = blocks[s]
    Cbd[...] = jnp.zeros_like(Cbd)
    zero = jnp.zeros((NC, RM), f32)
    row = lax.broadcasted_iota(jnp.int32, (NC, RM), 0)
    for s in range(SD):
        crow[:, s * RM : (s + 1) * RM] = jnp.where(row == 6, float(s), cpad[s])
    for q in range(SD // 2):
        top = jnp.concatenate([cpad[2 * q], zero], axis=1)
        low = jnp.concatenate([zero, cpad[2 * q + 1]], axis=1)
        Cbd[2 * q * NC : (2 * q + 2) * NC, 2 * q * RM : (2 * q + 2) * RM] = jnp.concatenate(
            [top, low], axis=0
        ).astype(bf16)

    pl.semaphore_wait(barrier, PEERS - 1 + SETS - 1)

    slots_and_send(0, resid)

    def mask_modes(c):
        cols = at(c, CAP)
        a = jnp.broadcast_to(slot[0:1, cols] // CAP, (NC, CAP))
        v = crow[:, cols]
        Xm[:, cols] = jnp.concatenate(
            [jnp.where(a == k, v, 0.0) for k in range(PEERS)], axis=0
        ).astype(bf16)

    loop(RD // CAP, mask_modes)
    csend[...] = dot(Xm[...], BT[...]).reshape(PEERS, NC, CAP)
    csend[:, 7:8, 0:NK] = jnp.broadcast_to(corner[0:1].reshape(1, 1, NK), (PEERS, 1, NK))
    others(lambda q: remote(5, csend.at[q], crecv.at[me], q).start())
    crecv[me] = swap_pairs(csend[me])
    crecv[me, 7:8, 0:NK] = corner[0:1]

    receive_rows(0, p)

    def first(c):
        cols = at(c, RM)
        jr[:, cols] = resid[:, cols] + live[0:1, cols] * p[:, cols]

    loop(RD // RM, first)

    copy_v.wait()
    apply(jr, V, 1.0)
    sum_start(0)
    slots_and_send(1, f)

    others(lambda q: arrival(5, crecv.at[q], q).wait_recv())
    others(lambda q: remote(5, csend.at[q], crecv.at[me], q).wait_send())

    def expand(j):
        blk = crecv[j]
        sub = jnp.broadcast_to(blk[6:7], (NC, CAP))
        for q in range(SD // 2):
            Ce[j, 2 * q * NC : (2 * q + 2) * NC, :] = jnp.concatenate(
                [jnp.where(sub == float(2 * q), blk, 0.0),
                 jnp.where(sub == float(2 * q + 1), blk, 0.0)], axis=0
            ).astype(bf16)
        unknown = lax.broadcasted_iota(jnp.int32, (NCO, NK), 0).astype(f32)
        OHT[:, at(j, NK)] = jnp.where(unknown == blk[7:8, 0:NK], 1.0, 0.0).astype(bf16)

    loop(PEERS, expand)

    receive_rows(1, p)

    def first_direction(c):
        cols = at(c, RM)
        d[:, cols] = live[0:1, cols] * (f[:, cols] + p[:, cols])

    loop(RD // RM, first_direction)

    copy_w.wait()
    coarse_start(0)
    apply(d, W, 2.0)
    sum_start(1)
    slots_and_send(2, f)
    square = coarse_solve(0)
    sum_middle(0, None)
    sum_middle(1, square)
    partners_coarse()
    energy = sum_end(0)
    alpha = energy / sum_end(1)
    receive_rows(2, p)

    def update(c):
        cols = at(c, RM)
        on = live[0:1, cols]
        al = alpha[:, 0:1]
        jf = f[:, cols] + p[:, cols]
        k = kd[:, cols]
        mult[:, cols] = al * d[:, cols]
        resid[:, cols] -= al * (on * (jf + k))
        jr[:, cols] -= al * (on * (2.0 * jf + k + pk[:, cols]))

    loop(RD // RM, update)

    apply(jr, V, 1.0)
    sum_start(2)
    slots_and_send(3, f)
    sum_middle(2, None)
    new = sum_end(2)
    receive_rows(3, p)
    beta = new / energy

    def next_direction(c):
        cols = at(c, RM)
        d[:, cols] = live[0:1, cols] * (f[:, cols] + p[:, cols]) + beta[:, 0:1] * d[:, cols]

    loop(RD // RM, next_direction)

    coarse_start(1)
    apply(d, W, 2.0)
    sum_start(3)
    slots_and_send(4, f)
    square = coarse_solve(1)
    sum_middle(3, square)
    alpha2 = new / sum_end(3)
    receive_rows(4, p)

    def last(c):
        cols = at(c, RM)
        al = alpha2[:, 0:1]
        mult[:, cols] += al * d[:, cols]
        resid[:, cols] -= al * (live[0:1, cols] * (f[:, cols] + p[:, cols] + kd[:, cols]))

    loop(RD // RM, last)


def body(
    jump_rhs, w_factor, s_factor, rigid_coarse_blocks, coarse_factor, slot_of_row, pair_counts,
    corner_map,
):
    slot = slot_of_row.reshape(1, RD)
    corner = jnp.pad(corner_map.astype(f32), ((0, 0), (0, 2)), constant_values=-1.0)
    corner = jnp.broadcast_to(corner.reshape(1, NK), (8, NK))
    vm = pl.BlockSpec(memory_space=pltpu.VMEM)
    hbm = pl.BlockSpec(memory_space=pl.ANY)
    sm = pl.BlockSpec(memory_space=pltpu.SMEM)
    V = pltpu.VMEM
    vec = V((L, RD), f32)
    return pl.pallas_call(
        kernel,
        out_shape=(jax.ShapeDtypeStruct((L, RD), f32),) * 2,
        in_specs=[vm, hbm, hbm, vm, vm, vm, sm, vm],
        out_specs=[vm, vm],
        scratch_shapes=[
            V((SD, RM, RM), bf16), V((SD, RM, RM), bf16), V((CAP, RD), bf16), V((RD, CAP), bf16),
            V((GROUP * L, RD), bf16), V((8, RD), f32), vec, vec, vec, vec, vec, vec,
            V((PEERS, L, CAP), f32), V((2, PEERS, L, CAP), f32), V((PEERS, NC, CAP), f32),
            V((PEERS, NC, CAP), f32), V((SD, NC, RM), f32), V((NC, RD), f32), V((NK, RD), bf16),
            V((PEERS, NK, CAP), bf16), V((NCO, PEERS * NK), bf16),
            V((2, L, NK), f32), V((2, PEERS, L, NK), f32), V((2 * L, PEERS * NK), bf16),
            V((L, PEERS * NK), f32), V((PEERS * L, CAP), bf16),
            V((4, 8, 128), f32), V((4, PEERS, 8, 128), f32), V((4, 8, 128), f32),
            V((4, SETS, 8, 128), f32), V((L, 128), f32),
            pltpu.SemaphoreType.DMA((2,)), pltpu.SemaphoreType.DMA((12, PEERS)),
            pltpu.SemaphoreType.DMA((12, PEERS)), pltpu.SemaphoreType.DMA((4, SETS)),
            pltpu.SemaphoreType.DMA((4, SETS)),
        ],
        compiler_params=pltpu.CompilerParams(
            collective_id=0, has_side_effects=True, vmem_limit_bytes=62 << 20
        ),
        cost_estimate=pl.CostEstimate(
            flops=60_000_000_000, bytes_accessed=20 << 20, transcendentals=0
        ),
    )(jump_rhs, w_factor, s_factor, rigid_coarse_blocks, coarse_factor, slot, pair_counts, corner)


def solution(mesh):
    each = ("set", "sub")
    return jax.shard_map(
        body,
        mesh=mesh,
        in_specs=(
            P(None, each), P(each, None, None), P(each, None, None), P(each, None, None),
            P("set", None), P(each), P(each, None), P(each, None),
        ),
        out_specs=(P(None, each), P(None, each)),
        check_vma=False,
    )
```

```python
import jax
import jax.numpy as jnp
from jax import lax
from jax.experimental import pallas as pl
from jax.experimental.pallas import tpu as pltpu
from jax.sharding import PartitionSpec as P

f32 = jnp.float32
bf16 = jnp.bfloat16
MESH = pl.DeviceIdType.MESH
HI = lax.Precision.HIGHEST

L = 32
PEERS = 32
SETS = 4
CAP = 256
RD = 8192
SD = 16
RM = 512
NC = 8
NK = SD * NC
NCO = 512
QS = NCO // NK
GROUP = 8
GROUPS = PEERS // GROUP

NT = (((1,), (1,)), ((), ()))


def dot(a, b):
    return jnp.dot(a, b, preferred_element_type=f32)


def dot_nt(a, b):
    return lax.dot_general(a, b, NT, preferred_element_type=f32)


def at(i, n):
    return pl.ds(pl.multiple_of(i * n, n), n)


def loop(n, f):
    def step(i, carry):
        f(i)
        return carry

    lax.fori_loop(0, n, step, 0)


def split(x):
    high = x.astype(bf16)
    return high, (x - high.astype(f32)).astype(bf16)


def kernel(
    jump, w_hbm, s_hbm, blocks, factor, slot, counts, corner,
    mult, resid,
    W, V, B, BT, Xm, live, jr, f, p, d, kd, pk,
    send, recv, csend, crecv, cpad, crow, Cbd, Ce, OHT,
    gsend, grecv, hsend, hrecv, back, pks, psend, precv, qsend, qrecv, acc,
    wsem, ssem, rsem, qssem, qrsem,
):
    st = lax.axis_index("set")
    me = lax.axis_index("sub")
    mg = me // GROUP

    copy_v = pltpu.make_async_copy(s_hbm, V, wsem.at[0])
    copy_w = pltpu.make_async_copy(w_hbm, W, wsem.at[1])
    copy_v.start()
    copy_w.start()

    barrier = pltpu.get_barrier_semaphore()

    def greet(k):
        pl.semaphore_signal(
            barrier, inc=1, device_id=(st, lax.rem(me + 1 + k, PEERS)), device_id_type=MESH
        )

    def greet_set(k):
        pl.semaphore_signal(
            barrier, inc=1, device_id=(lax.rem(st + 1 + k, SETS), me), device_id_type=MESH
        )

    loop(PEERS - 1, greet)
    loop(SETS - 1, greet_set)

    def remote(e, src, dst, q):
        return pltpu.make_async_remote_copy(
            src_ref=src, dst_ref=dst, send_sem=ssem.at[e, q], recv_sem=rsem.at[e, me],
            device_id=(st, q), device_id_type=MESH,
        )

    def arrival(e, dst, q):
        return pltpu.make_async_remote_copy(
            src_ref=dst, dst_ref=dst, send_sem=ssem.at[e, q], recv_sem=rsem.at[e, q],
            device_id=(st, q), device_id_type=MESH,
        )

    def others(f):
        def one(k):
            f(lax.rem(me + 1 + k, PEERS))

        loop(PEERS - 1, one)

    def group_others(g, f):
        def one(k):
            q = g * GROUP + lax.rem(me + k, GROUP)

            @pl.when(q != me)
            def _():
                f(q)

        loop(GROUP, one)

    def plane(i):
        return jnp.where(i == 0, 2, jnp.where(i == 3, 0, 2 * i - 1))

    def swap_pairs(x):
        lane = lax.broadcasted_iota(jnp.int32, x.shape, 1)
        n = x.shape[1]
        return jnp.where(lane % 2 == 0, pltpu.roll(x, n - 1, 1), pltpu.roll(x, 1, 1))

    def slots_and_send(e, x):
        def one(i):
            g = lax.rem(mg + plane(i), GROUPS)
            for c in range(RD // CAP):
                cols = slice(c * CAP, (c + 1) * CAP)
                a = jnp.broadcast_to(slot[0:1, cols] // CAP - g * GROUP, (L, CAP))
                v = x[:, cols]
                Xm[:, cols] = jnp.concatenate(
                    [jnp.where(a == k, v, 0.0).astype(bf16) for k in range(GROUP)], axis=0
                )
            send[pl.ds(g * GROUP, GROUP)] = dot(Xm[...], BT[...]).reshape(GROUP, L, CAP)
            group_others(g, lambda q: remote(e, send.at[q], recv.at[e % 2, me], q).start())

        loop(GROUPS, one)
        recv[e % 2, me] = swap_pairs(send[me])

    def sent(e):
        others(lambda q: remote(e, send.at[q], recv.at[e % 2, me], q).wait_send())

    def rows_of_group(g, blocks16, out, first):
        for c in range(RD // CAP):
            cols = slice(c * CAP, (c + 1) * CAP)
            a = jnp.broadcast_to(slot[0:1, cols] // CAP - g * GROUP, (L, CAP))
            u = dot(blocks16, B[:, cols])
            res = out[:, cols]
            for k in range(GROUP):
                res = jnp.where(a == k, u[k * L : (k + 1) * L], res)
            out[:, cols] = res

    def receive_rows(e, out):
        out[...] = jnp.zeros_like(out)

        def one(i):
            g = lax.rem(mg + GROUPS - plane(i), GROUPS)
            group_others(g, lambda q: arrival(e, recv.at[e % 2, q], q).wait_recv())
            blk = recv[e % 2, pl.ds(g * GROUP, GROUP)].reshape(GROUP * L, CAP).astype(bf16)
            rows_of_group(g, blk, out, False)

        loop(GROUPS, one)
        sent(e)

    def gram(F):
        def one(s):
            m = F[s]
            F[s] = dot_nt(m, m).astype(bf16)

        loop(SD, one)

    def apply(x, F, scale):
        acc[...] = jnp.zeros_like(acc)

        def one(i):
            for k in range(4):
                s = i * 4 + k
                cols = at(s, RM)
                v = x[:, cols] * scale
                out = dot(v.astype(bf16), F[s])
                f[:, cols] = out
                prod = v * out
                acc[...] += sum(prod[:, n * 128 : (n + 1) * 128] for n in range(RM // 128))

        loop(SD // 4, one)

    def lanes_to_row(x):
        x = jnp.concatenate([x, jnp.zeros((128 - L, 128), f32)], axis=0)
        return jnp.sum(x.T, axis=0, keepdims=True)

    def row_to_column(x):
        return jnp.broadcast_to(x, (128, 128)).T[0:L]

    def sum_start(e):
        psend[e] = lanes_to_row(acc[...])
        precv[e, me] = psend[e]
        others(lambda q: remote(8 + e, psend.at[e], precv.at[e, me], q).start())

    def across(e, q):
        return pltpu.make_async_remote_copy(
            src_ref=qsend.at[e], dst_ref=qrecv.at[e, st], send_sem=qssem.at[e, q],
            recv_sem=qrsem.at[e, st], device_id=(q, me), device_id_type=MESH,
        )

    def across_arrival(e, q):
        return pltpu.make_async_remote_copy(
            src_ref=qsend.at[e], dst_ref=qrecv.at[e, q], send_sem=qssem.at[e, q],
            recv_sem=qrsem.at[e, q], device_id=(q, me), device_id_type=MESH,
        )

    def other_sets(f):
        loop(SETS - 1, lambda k: f(lax.rem(st + 1 + k, SETS)))

    def sum_middle(e, extra):
        others(lambda q: arrival(8 + e, precv.at[e, q], q).wait_recv())
        others(lambda q: remote(8 + e, psend.at[e], precv.at[e, me], q).wait_send())
        total = jnp.sum(precv[e], axis=0)
        if extra is not None:
            total = total + extra
        qsend[e] = total
        qrecv[e, st] = total
        other_sets(lambda q: across(e, q).start())

    def sum_end(e):
        other_sets(lambda q: across_arrival(e, q).wait_recv())
        other_sets(lambda q: across(e, q).wait_send())
        return row_to_column(jnp.sum(qrecv[e], axis=0))

    def coarse_start(e):
        g = dot_nt(d[...].astype(bf16), Cbd[...])
        unknown = lax.broadcasted_iota(jnp.int32, (NK, NK), 0)
        hits = jnp.concatenate(
            [jnp.where((unknown + q * NK).astype(f32) == corner[0:1], 1.0, 0.0).astype(bf16)
             for q in range(QS)], axis=1
        )

        def spread(x):
            zero = jnp.zeros((L, NK), bf16)
            return jnp.concatenate(
                [jnp.concatenate([x if r == q else zero for r in range(QS)], axis=1)
                 for q in range(QS)], axis=0
            )

        high, low = split(g)
        x = dot_nt(hits, spread(high)) + dot_nt(hits, spread(low))
        for j in range(PEERS):
            gsend[e, j] = x[j * QS : (j + 1) * QS]
        grecv[e, me] = gsend[e, me]
        others(lambda q: remote(6 + e, gsend.at[e, q], grecv.at[e, me], q).start())

    def coarse_sum(e):
        others(lambda q: arrival(6 + e, grecv.at[e, q], q).wait_recv())
        hsend[e] = jnp.sum(grecv[e], axis=0)
        hrecv[e, me] = hsend[e]
        others(lambda q: remote(12 + e, hsend.at[e], hrecv.at[e, me], q).start())
        others(lambda q: remote(6 + e, gsend.at[e, q], grecv.at[e, me], q).wait_send())

    def coarse_solve(e):
        others(lambda q: arrival(12 + e, hrecv.at[e, q], q).wait_recv())
        others(lambda q: remote(12 + e, hsend.at[e], hrecv.at[e, me], q).wait_send())
        x = jnp.concatenate([hrecv[e, j] for j in range(PEERS)], axis=0).T
        coarse_in = jnp.concatenate([x[q * L : (q + 1) * L] for q in range(QS)], axis=1)
        middle = jnp.dot(coarse_in, factor[...], precision=HI, preferred_element_type=f32)
        sol = lax.dot_general(
            middle, factor[...], NT, precision=HI, preferred_element_type=f32
        )
        both = dot(jnp.concatenate(split(sol), axis=0), OHT[...])
        back[...] = both[:L] + both[L:]
        kd[...] = dot(back[:, at(me, NK)].astype(bf16), Cbd[...])
        square = middle * middle
        return lanes_to_row(sum(square[:, n * 128 : (n + 1) * 128] for n in range(NCO // 128)))

    def partners_coarse():
        def one(j):
            pks[pl.ds(pl.multiple_of(j * L, L), L), :] = dot(
                back[:, at(j, NK)].astype(bf16), Ce[j]
            ).astype(bf16)

        loop(PEERS, one)
        pk[...] = jnp.zeros_like(pk)
        loop(
            GROUPS,
            lambda g: rows_of_group(g, pks[at(g, GROUP * L), :], pk, False),
        )

    def onehot(c):
        cols = at(c, CAP)
        hit = lax.broadcasted_iota(jnp.int32, (CAP, CAP), 0) == slot[0:1, cols] % CAP
        m = jnp.where(hit, 1.0, 0.0)
        B[:, cols] = m.astype(bf16)
        BT[cols, :] = m.T.astype(bf16)

    loop(RD // CAP, onehot)

    def live_rows(c):
        cols = at(c, RM)
        s = slot[0:1, cols]
        a = s // CAP
        n = jnp.zeros_like(s)
        for k in range(PEERS):
            n = jnp.where(a == k, counts[0, k], n)
        on = jnp.where(s % CAP < n, 1.0, 0.0)
        live[:, cols] = jnp.broadcast_to(on, (8, RM))
        resid[:, cols] = on * jump[:, cols]

    loop(RD // RM, live_rows)

    cpad[...] = jnp.zeros_like(cpad)
    for s in range(SD):
        for k in range(6):
            cpad[s, k : k + 1, :] = blocks[k, s : s + 1, :]
    Cbd[...] = jnp.zeros_like(Cbd)
    zero = jnp.zeros((NC, RM), f32)
    row = lax.broadcasted_iota(jnp.int32, (NC, RM), 0)
    for s in range(SD):
        crow[:, s * RM : (s + 1) * RM] = jnp.where(row == 6, float(s), cpad[s])
    for q in range(SD // 2):
        top = jnp.concatenate([cpad[2 * q], zero], axis=1)
        low = jnp.concatenate([zero, cpad[2 * q + 1]], axis=1)
        Cbd[2 * q * NC : (2 * q + 2) * NC, 2 * q * RM : (2 * q + 2) * RM] = jnp.concatenate(
            [top, low], axis=0
        ).astype(bf16)

    pl.semaphore_wait(barrier, PEERS - 1 + SETS - 1)

    slots_and_send(0, resid)

    def mask_modes(c):
        cols = at(c, CAP)
        a = jnp.broadcast_to(slot[0:1, cols] // CAP, (NC, CAP))
        v = crow[:, cols]
        Xm[:, cols] = jnp.concatenate(
            [jnp.where(a == k, v, 0.0) for k in range(PEERS)], axis=0
        ).astype(bf16)

    loop(RD // CAP, mask_modes)
    csend[...] = dot(Xm[...], BT[...]).reshape(PEERS, NC, CAP)
    csend[:, 7:8, 0:NK] = jnp.broadcast_to(corner[0:1].reshape(1, 1, NK), (PEERS, 1, NK))
    crecv[me] = swap_pairs(csend[me])
    crecv[me, 7:8, 0:NK] = corner[0:1]

    copy_v.wait()
    gram(V)
    receive_rows(0, p)
    others(lambda q: remote(5, csend.at[q], crecv.at[me], q).start())

    def first(c):
        cols = at(c, RM)
        jr[:, cols] = resid[:, cols] + live[0:1, cols] * p[:, cols]

    loop(RD // RM, first)

    apply(jr, V, 1.0)
    sum_start(0)
    slots_and_send(1, f)

    others(lambda q: arrival(5, crecv.at[q], q).wait_recv())
    others(lambda q: remote(5, csend.at[q], crecv.at[me], q).wait_send())

    def expand(j):
        blk = crecv[j]
        sub = jnp.broadcast_to(blk[6:7], (NC, CAP))
        for q in range(SD // 2):
            Ce[j, 2 * q * NC : (2 * q + 2) * NC, :] = jnp.concatenate(
                [jnp.where(sub == float(2 * q), blk, 0.0),
                 jnp.where(sub == float(2 * q + 1), blk, 0.0)], axis=0
            ).astype(bf16)
        unknown = lax.broadcasted_iota(jnp.int32, (NCO, NK), 0).astype(f32)
        OHT[:, at(j, NK)] = jnp.where(unknown == blk[7:8, 0:NK], 1.0, 0.0).astype(bf16)

    loop(PEERS, expand)
    copy_w.wait()
    gram(W)

    receive_rows(1, p)

    def first_direction(c):
        cols = at(c, RM)
        d[:, cols] = live[0:1, cols] * (f[:, cols] + p[:, cols])

    loop(RD // RM, first_direction)

    coarse_start(0)
    apply(d, W, 2.0)
    sum_start(1)
    slots_and_send(2, f)
    coarse_sum(0)
    square = coarse_solve(0)
    sum_middle(0, None)
    sum_middle(1, square)
    partners_coarse()
    energy = sum_end(0)
    alpha = energy / sum_end(1)
    receive_rows(2, p)

    def update(c):
        cols = at(c, RM)
        on = live[0:1, cols]
        al = alpha[:, 0:1]
        jf = f[:, cols] + p[:, cols]
        k = kd[:, cols]
        mult[:, cols] = al * d[:, cols]
        resid[:, cols] -= al * (on * (jf + k))
        jr[:, cols] -= al * (on * (2.0 * jf + k + pk[:, cols]))

    loop(RD // RM, update)

    apply(jr, V, 1.0)
    sum_start(2)
    slots_and_send(3, f)
    sum_middle(2, None)
    new = sum_end(2)
    receive_rows(3, p)
    beta = new / energy

    def next_direction(c):
        cols = at(c, RM)
        d[:, cols] = live[0:1, cols] * (f[:, cols] + p[:, cols]) + beta[:, 0:1] * d[:, cols]

    loop(RD // RM, next_direction)

    coarse_start(1)
    apply(d, W, 2.0)
    sum_start(3)
    slots_and_send(4, f)
    coarse_sum(1)
    square = coarse_solve(1)
    sum_middle(3, square)
    alpha2 = new / sum_end(3)
    receive_rows(4, p)

    def last(c):
        cols = at(c, RM)
        al = alpha2[:, 0:1]
        mult[:, cols] += al * d[:, cols]
        resid[:, cols] -= al * (live[0:1, cols] * (f[:, cols] + p[:, cols] + kd[:, cols]))

    loop(RD // RM, last)


def body(
    jump_rhs, w_factor, s_factor, rigid_coarse_blocks, coarse_factor, slot_of_row, pair_counts,
    corner_map,
):
    slot = slot_of_row.reshape(1, RD)
    corner = jnp.pad(corner_map.astype(f32), ((0, 0), (0, 2)), constant_values=-1.0)
    corner = corner.reshape(1, NK)
    rigid_coarse_blocks = jnp.transpose(rigid_coarse_blocks, (1, 0, 2))
    vm = pl.BlockSpec(memory_space=pltpu.VMEM)
    hbm = pl.BlockSpec(memory_space=pl.ANY)
    sm = pl.BlockSpec(memory_space=pltpu.SMEM)
    V = pltpu.VMEM
    vec = V((L, RD), f32)
    return pl.pallas_call(
        kernel,
        out_shape=(jax.ShapeDtypeStruct((L, RD), f32),) * 2,
        in_specs=[vm, hbm, hbm, vm, vm, vm, sm, vm],
        out_specs=[vm, vm],
        scratch_shapes=[
            V((SD, RM, RM), bf16), V((SD, RM, RM), bf16), V((CAP, RD), bf16), V((RD, CAP), bf16),
            V((GROUP * L, RD), bf16), V((8, RD), f32), vec, vec, vec, vec, vec, vec,
            V((PEERS, L, CAP), f32), V((2, PEERS, L, CAP), f32), V((PEERS, NC, CAP), f32),
            V((PEERS, NC, CAP), f32), V((SD, NC, RM), f32), V((NC, RD), f32), V((NK, RD), bf16),
            V((PEERS, NK, CAP), bf16), V((NCO, PEERS * NK), bf16),
            V((2, PEERS, QS, NK), f32), V((2, PEERS, QS, NK), f32), V((2, QS, NK), f32),
            V((2, PEERS, QS, NK), f32),
            V((L, PEERS * NK), f32), V((PEERS * L, CAP), bf16),
            V((4, 1, 128), f32), V((4, PEERS, 1, 128), f32), V((4, 1, 128), f32),
            V((4, SETS, 1, 128), f32), V((L, 128), f32),
            pltpu.SemaphoreType.DMA((2,)), pltpu.SemaphoreType.DMA((14, PEERS)),
            pltpu.SemaphoreType.DMA((14, PEERS)), pltpu.SemaphoreType.DMA((4, SETS)),
            pltpu.SemaphoreType.DMA((4, SETS)),
        ],
        compiler_params=pltpu.CompilerParams(
            collective_id=0, has_side_effects=True, vmem_limit_bytes=62 << 20
        ),
        cost_estimate=pl.CostEstimate(
            flops=60_000_000_000, bytes_accessed=20 << 20, transcendentals=0
        ),
    )(jump_rhs, w_factor, s_factor, rigid_coarse_blocks, coarse_factor, slot, pair_counts, corner)


def solution(mesh):
    each = ("set", "sub")
    return jax.shard_map(
        body,
        mesh=mesh,
        in_specs=(
            P(None, each), P(each, None, None), P(each, None, None), P(each, None, None),
            P("set", None), P(each), P(each, None), P(each, None),
        ),
        out_specs=(P(None, each), P(None, each)),
        check_vma=False,
    )
```

```python
import jax
import jax.numpy as jnp
from jax import lax
from jax.experimental import pallas as pl
from jax.experimental.pallas import tpu as pltpu
from jax.sharding import PartitionSpec as P

f32 = jnp.float32
bf16 = jnp.bfloat16
MESH = pl.DeviceIdType.MESH
HI = lax.Precision.HIGHEST

L = 32
PEERS = 32
SETS = 4
CAP = 256
RD = 8192
SD = 16
RM = 512
NC = 8
NK = SD * NC
NCO = 512
QS = NCO // NK
GROUP = 8
GROUPS = PEERS // GROUP

NT = (((1,), (1,)), ((), ()))


def dot(a, b):
    return jnp.dot(a, b, preferred_element_type=f32)


def dot_nt(a, b):
    return lax.dot_general(a, b, NT, preferred_element_type=f32)


def at(i, n):
    return pl.ds(pl.multiple_of(i * n, n), n)


def loop(n, f):
    def step(i, carry):
        f(i)
        return carry

    lax.fori_loop(0, n, step, 0)


def split(x):
    high = x.astype(bf16)
    return high, (x - high.astype(f32)).astype(bf16)


def kernel(
    jump, w_hbm, s_hbm, blocks, factor, slot, counts, corner,
    mult, resid,
    W, V, B, BT, Xm, live, jr, f, p, d, kd, pk,
    send, recv, csend, crecv, cpad, crow, Cbd, Ce, OHT,
    gsend, grecv, hsend, hrecv, back, pks, psend, precv, qsend, qrecv, acc, acc0,
    sa, wsem, assem, arsem, ssem, rsem, qssem, qrsem,
):
    st = lax.axis_index("set")
    me = lax.axis_index("sub")
    mg = me // GROUP

    copy_v = pltpu.make_async_copy(s_hbm, V, wsem.at[0])
    copy_w = pltpu.make_async_copy(w_hbm, W, wsem.at[1])
    copy_v.start()
    copy_w.start()

    barrier = pltpu.get_barrier_semaphore()

    def greet(k):
        pl.semaphore_signal(
            barrier, inc=1, device_id=(st, lax.rem(me + 1 + k, PEERS)), device_id_type=MESH
        )

    def greet_set(k):
        pl.semaphore_signal(
            barrier, inc=1, device_id=(lax.rem(st + 1 + k, SETS), me), device_id_type=MESH
        )

    loop(PEERS - 1, greet)
    loop(SETS - 1, greet_set)

    def wrap(q):
        return jnp.where(q >= PEERS, q - PEERS, q)

    def others(f):
        for k in range(1, PEERS):
            f(wrap(me + k))

    def send_all(n, src, dst):
        others(
            lambda q: pltpu.make_async_remote_copy(
                src_ref=src(q), dst_ref=dst, send_sem=ssem.at[n], recv_sem=rsem.at[n],
                device_id=(st, q), device_id_type=MESH,
            ).start()
        )

    def wait_all(n, dst):
        copy = pltpu.make_async_remote_copy(
            src_ref=dst, dst_ref=dst, send_sem=ssem.at[n], recv_sem=rsem.at[n],
            device_id=(st, wrap(me + 1)), device_id_type=MESH,
        )
        copy.wait_recv()
        copy.wait_send()

    def block_copy(e, src, dst, g, q):
        return pltpu.make_async_remote_copy(
            src_ref=src, dst_ref=dst, send_sem=assem.at[e], recv_sem=arsem.at[e, g],
            device_id=(st, q), device_id_type=MESH,
        )

    def send_group(e, g):
        for k in range(GROUP):
            r = lax.rem(me, GROUP) + k
            q = g * GROUP + jnp.where(r >= GROUP, r - GROUP, r)

            @pl.when(q != me)
            def _():
                block_copy(e, send.at[q], recv.at[e % 2, me], mg, q).start()

    def wait_group(e, g, n):
        some = recv.at[e % 2, pl.ds(g * GROUP, n)]
        block_copy(e, some, some, g, wrap(me + 1)).wait_recv()

    def plane(i):
        return jnp.where(i == 0, 2, jnp.where(i == 3, 0, 2 * i - 1))

    def swap_pairs(x):
        lane = lax.broadcasted_iota(jnp.int32, x.shape, 1)
        n = x.shape[1]
        return jnp.where(lane % 2 == 0, pltpu.roll(x, n - 1, 1), pltpu.roll(x, 1, 1))

    def slots_and_send(e, x, early=None):
        def one(i):
            g = lax.rem(mg + plane(i), GROUPS)
            for c in range(RD // CAP):
                cols = slice(c * CAP, (c + 1) * CAP)
                a = jnp.concatenate([sa[:, cols] - g * GROUP] * (L // 8), axis=0)
                v = x[:, cols]
                Xm[:, cols] = jnp.concatenate(
                    [jnp.where(a == k, v, 0.0).astype(bf16) for k in range(GROUP)], axis=0
                )
            send[pl.ds(g * GROUP, GROUP)] = dot(Xm[...], BT[...]).reshape(GROUP, L, CAP)
            if early is not None:
                pl.when(i == 0)(early)
            send_group(e, g)

        loop(GROUPS, one)
        recv[e % 2, me] = swap_pairs(send[me])

    def sent(e):
        most = send.at[pl.ds(0, PEERS - 1)]
        block_copy(e, most, most, mg, wrap(me + 1)).wait_send()

    def rows_of_group(g, blocks16, out, first):
        for c in range(RD // CAP):
            cols = slice(c * CAP, (c + 1) * CAP)
            a = jnp.concatenate([sa[:, cols] - g * GROUP] * (L // 8), axis=0)
            u = dot(blocks16, B[:, cols])
            res = out[:, cols]
            for k in range(GROUP):
                res = jnp.where(a == k, u[k * L : (k + 1) * L], res)
            out[:, cols] = res

    def receive_rows(e, out):
        out[...] = jnp.zeros_like(out)

        def one(i):
            g = lax.rem(mg + GROUPS - plane(i), GROUPS)
            pl.when(i < GROUPS - 1)(lambda: wait_group(e, g, GROUP))
            pl.when(i == GROUPS - 1)(lambda: wait_group(e, g, GROUP - 1))
            blk = recv[e % 2, pl.ds(g * GROUP, GROUP)].reshape(GROUP * L, CAP).astype(bf16)
            rows_of_group(g, blk, out, False)

        loop(GROUPS, one)
        sent(e)

    def gram(F):
        def one(s):
            m = F[s]
            F[s] = dot_nt(m, m).astype(bf16)

        loop(SD, one)

    def apply(x, F, scale):
        acc[...] = jnp.zeros_like(acc)

        def one(i):
            for k in range(4):
                s = i * 4 + k
                cols = at(s, RM)
                v = x[:, cols] * scale
                out = dot(v.astype(bf16), F[s])
                f[:, cols] = out
                prod = v * out
                acc[...] += sum(prod[:, n * 128 : (n + 1) * 128] for n in range(RM // 128))

        loop(SD // 4, one)

    def lanes_to_row(x):
        x = jnp.concatenate([x, jnp.zeros((128 - L, 128), f32)], axis=0)
        return jnp.sum(x.T, axis=0, keepdims=True)

    def row_to_column(x):
        return jnp.broadcast_to(x, (128, 128)).T[0:L]

    def sum_start():
        psend[0] = lanes_to_row(acc[...])
        precv[me] = psend[0]
        send_all(5, lambda q: psend.at[0], precv.at[me])

    def sum_middle():
        wait_all(5, precv.at[pl.ds(0, PEERS - 1)])
        sum_out(1, jnp.sum(precv[...], axis=0))

    def across(e, q):
        return pltpu.make_async_remote_copy(
            src_ref=qsend.at[e], dst_ref=qrecv.at[e, st], send_sem=qssem.at[e, q],
            recv_sem=qrsem.at[e, st], device_id=(q, me), device_id_type=MESH,
        )

    def across_arrival(e, q):
        return pltpu.make_async_remote_copy(
            src_ref=qsend.at[e], dst_ref=qrecv.at[e, q], send_sem=qssem.at[e, q],
            recv_sem=qrsem.at[e, q], device_id=(q, me), device_id_type=MESH,
        )

    def other_sets(f):
        loop(SETS - 1, lambda k: f(lax.rem(st + 1 + k, SETS)))

    def sum_out(e, total):
        total = jnp.concatenate([total, jnp.zeros((8 - total.shape[0], 128), f32)], axis=0)
        qsend[e] = total
        qrecv[e, st] = total
        other_sets(lambda q: across(e, q).start())

    def sum_end(e, n):
        other_sets(lambda q: across_arrival(e, q).wait_recv())
        other_sets(lambda q: across(e, q).wait_send())
        total = jnp.sum(qrecv[e], axis=0)
        return [row_to_column(total[r : r + 1]) for r in range(n)]

    def coarse_start(e):
        g = dot_nt(d[...].astype(bf16), Cbd[...])
        unknown = lax.broadcasted_iota(jnp.int32, (NK, NK), 0)
        hits = jnp.concatenate(
            [jnp.where((unknown + q * NK).astype(f32) == corner[0:1], 1.0, 0.0).astype(bf16)
             for q in range(QS)], axis=1
        )

        def spread(x):
            zero = jnp.zeros((L, NK), bf16)
            return jnp.concatenate(
                [jnp.concatenate([x if r == q else zero for r in range(QS)], axis=1)
                 for q in range(QS)], axis=0
            )

        high, low = split(g)
        x = dot_nt(hits, spread(high)) + dot_nt(hits, spread(low))
        for j in range(PEERS):
            gsend[e, j] = x[j * QS : (j + 1) * QS]
        grecv[e, me] = gsend[e, me]
        send_all(1 + e, lambda q: gsend.at[e, q], grecv.at[e, me])

    def coarse_sum(e):
        wait_all(1 + e, grecv.at[e, pl.ds(0, PEERS - 1)])
        hsend[e, 0:QS] = jnp.sum(grecv[e], axis=0)
        hsend[e, QS : QS + 1] = lanes_to_row(acc[...])
        hsend[e, QS + 1 : QS + 2] = lanes_to_row(acc0[...])
        hrecv[e, me] = hsend[e]
        send_all(3 + e, lambda q: hsend.at[e], hrecv.at[e, me])

    def coarse_solve(e):
        wait_all(3 + e, hrecv.at[e, pl.ds(0, PEERS - 1)])
        x = jnp.concatenate([hrecv[e, j, 0:QS] for j in range(PEERS)], axis=0).T
        sums = jnp.sum(hrecv[e, :, QS : QS + 2], axis=0)
        coarse_in = jnp.concatenate([x[q * L : (q + 1) * L] for q in range(QS)], axis=1)
        middle = jnp.dot(coarse_in, factor[...], precision=HI, preferred_element_type=f32)
        sol = lax.dot_general(
            middle, factor[...], NT, precision=HI, preferred_element_type=f32
        )
        both = dot(jnp.concatenate(split(sol), axis=0), OHT[...])
        back[...] = both[:L] + both[L:]
        kd[...] = dot(back[:, at(me, NK)].astype(bf16), Cbd[...])
        square = middle * middle
        square = lanes_to_row(sum(square[:, n * 128 : (n + 1) * 128] for n in range(NCO // 128)))
        sum_out(2 * e, jnp.concatenate([sums[0:1] + square, sums[1:2]], axis=0))

    def partners_coarse():
        def one(j):
            pks[pl.ds(pl.multiple_of(j * L, L), L), :] = dot(
                back[:, at(j, NK)].astype(bf16), Ce[j]
            ).astype(bf16)

        loop(PEERS, one)
        pk[...] = jnp.zeros_like(pk)
        loop(
            GROUPS,
            lambda g: rows_of_group(g, pks[at(g, GROUP * L), :], pk, False),
        )

    def onehot(c):
        cols = at(c, CAP)
        hit = lax.broadcasted_iota(jnp.int32, (CAP, CAP), 0) == slot[0:1, cols] % CAP
        m = jnp.where(hit, 1.0, 0.0)
        B[:, cols] = m.astype(bf16)
        BT[cols, :] = m.T.astype(bf16)

    loop(RD // CAP, onehot)

    def live_rows(c):
        cols = at(c, RM)
        s = slot[0:1, cols]
        a = s // CAP
        sa[:, cols] = jnp.broadcast_to(a, (8, RM))
        n = jnp.zeros_like(s)
        for k in range(PEERS):
            n = jnp.where(a == k, counts[0, k], n)
        on = jnp.where(s % CAP < n, 1.0, 0.0)
        live[:, cols] = jnp.broadcast_to(on, (8, RM))
        resid[:, cols] = on * jump[:, cols]

    loop(RD // RM, live_rows)

    cpad[...] = jnp.zeros_like(cpad)
    for s in range(SD):
        for k in range(6):
            cpad[s, k : k + 1, :] = blocks[k, s : s + 1, :]
    Cbd[...] = jnp.zeros_like(Cbd)
    zero = jnp.zeros((NC, RM), f32)
    row = lax.broadcasted_iota(jnp.int32, (NC, RM), 0)
    for s in range(SD):
        crow[:, s * RM : (s + 1) * RM] = jnp.where(row == 6, float(s), cpad[s])
    for q in range(SD // 2):
        top = jnp.concatenate([cpad[2 * q], zero], axis=1)
        low = jnp.concatenate([zero, cpad[2 * q + 1]], axis=1)
        Cbd[2 * q * NC : (2 * q + 2) * NC, 2 * q * RM : (2 * q + 2) * RM] = jnp.concatenate(
            [top, low], axis=0
        ).astype(bf16)

    pl.semaphore_wait(barrier, PEERS - 1 + SETS - 1)

    slots_and_send(0, resid)

    def mask_modes(c):
        cols = at(c, CAP)
        a = sa[:, cols]
        v = crow[:, cols]
        Xm[:, cols] = jnp.concatenate(
            [jnp.where(a == k, v, 0.0) for k in range(PEERS)], axis=0
        ).astype(bf16)

    loop(RD // CAP, mask_modes)
    csend[...] = dot(Xm[...], BT[...]).reshape(PEERS, NC, CAP)
    csend[:, 7:8, 0:NK] = jnp.broadcast_to(corner[0:1].reshape(1, 1, NK), (PEERS, 1, NK))
    crecv[me] = swap_pairs(csend[me])
    crecv[me, 7:8, 0:NK] = corner[0:1]

    copy_v.wait()
    gram(V)
    receive_rows(0, p)
    send_all(0, lambda q: csend.at[q], crecv.at[me])

    def first(c):
        cols = at(c, RM)
        jr[:, cols] = resid[:, cols] + live[0:1, cols] * p[:, cols]

    loop(RD // RM, first)

    apply(jr, V, 1.0)
    acc0[...] = acc[...]
    slots_and_send(1, f)

    wait_all(0, crecv.at[pl.ds(0, PEERS - 1)])

    def expand(j):
        blk = crecv[j]
        sub = jnp.broadcast_to(blk[6:7], (NC, CAP))
        for q in range(SD // 2):
            Ce[j, 2 * q * NC : (2 * q + 2) * NC, :] = jnp.concatenate(
                [jnp.where(sub == float(2 * q), blk, 0.0),
                 jnp.where(sub == float(2 * q + 1), blk, 0.0)], axis=0
            ).astype(bf16)
        unknown = lax.broadcasted_iota(jnp.int32, (NCO, NK), 0).astype(f32)
        OHT[:, at(j, NK)] = jnp.where(unknown == blk[7:8, 0:NK], 1.0, 0.0).astype(bf16)

    loop(PEERS, expand)
    copy_w.wait()
    gram(W)

    receive_rows(1, p)

    def first_direction(c):
        cols = at(c, RM)
        d[:, cols] = live[0:1, cols] * (f[:, cols] + p[:, cols])

    loop(RD // RM, first_direction)

    coarse_start(0)
    apply(d, W, 2.0)
    slots_and_send(2, f, lambda: coarse_sum(0))
    coarse_solve(0)
    partners_coarse()
    receive_rows(2, p)
    curvature, energy = sum_end(0, 2)
    alpha = energy / curvature

    def update(c):
        cols = at(c, RM)
        on = live[0:1, cols]
        al = alpha[:, 0:1]
        jf = f[:, cols] + p[:, cols]
        k = kd[:, cols]
        mult[:, cols] = al * d[:, cols]
        resid[:, cols] -= al * (on * (jf + k))
        jr[:, cols] -= al * (on * (2.0 * jf + k + pk[:, cols]))

    loop(RD // RM, update)

    apply(jr, V, 1.0)
    sum_start()
    slots_and_send(3, f)
    sum_middle()
    receive_rows(3, p)
    (new,) = sum_end(1, 1)
    beta = new / energy

    def next_direction(c):
        cols = at(c, RM)
        d[:, cols] = live[0:1, cols] * (f[:, cols] + p[:, cols]) + beta[:, 0:1] * d[:, cols]

    loop(RD // RM, next_direction)

    coarse_start(1)
    apply(d, W, 2.0)
    slots_and_send(4, f, lambda: coarse_sum(1))
    coarse_solve(1)
    receive_rows(4, p)
    (curvature,) = sum_end(2, 1)
    alpha2 = new / curvature

    def last(c):
        cols = at(c, RM)
        al = alpha2[:, 0:1]
        mult[:, cols] += al * d[:, cols]
        resid[:, cols] -= al * (live[0:1, cols] * (f[:, cols] + p[:, cols] + kd[:, cols]))

    loop(RD // RM, last)


def body(
    jump_rhs, w_factor, s_factor, rigid_coarse_blocks, coarse_factor, slot_of_row, pair_counts,
    corner_map,
):
    slot = slot_of_row.reshape(1, RD)
    corner = jnp.pad(corner_map.astype(f32), ((0, 0), (0, 2)), constant_values=-1.0)
    corner = corner.reshape(1, NK)
    rigid_coarse_blocks = jnp.transpose(rigid_coarse_blocks, (1, 0, 2))
    vm = pl.BlockSpec(memory_space=pltpu.VMEM)
    hbm = pl.BlockSpec(memory_space=pl.ANY)
    sm = pl.BlockSpec(memory_space=pltpu.SMEM)
    V = pltpu.VMEM
    vec = V((L, RD), f32)
    return pl.pallas_call(
        kernel,
        out_shape=(jax.ShapeDtypeStruct((L, RD), f32),) * 2,
        in_specs=[vm, hbm, hbm, vm, vm, vm, sm, vm],
        out_specs=[vm, vm],
        scratch_shapes=[
            V((SD, RM, RM), bf16), V((SD, RM, RM), bf16), V((CAP, RD), bf16), V((RD, CAP), bf16),
            V((GROUP * L, RD), bf16), V((8, RD), f32), vec, vec, vec, vec, vec, vec,
            V((PEERS, L, CAP), f32), V((2, PEERS, L, CAP), f32), V((PEERS, NC, CAP), f32),
            V((PEERS, NC, CAP), f32), V((SD, NC, RM), f32), V((NC, RD), f32), V((NK, RD), bf16),
            V((PEERS, NK, CAP), bf16), V((NCO, PEERS * NK), bf16),
            V((2, PEERS, QS, NK), f32), V((2, PEERS, QS, NK), f32), V((2, 8, NK), f32),
            V((2, PEERS, 8, NK), f32),
            V((L, PEERS * NK), f32), V((PEERS * L, CAP), bf16),
            V((1, 1, 128), f32), V((PEERS, 1, 128), f32), V((3, 8, 128), f32),
            V((3, SETS, 8, 128), f32), V((L, 128), f32), V((L, 128), f32), V((8, RD), jnp.int32),
            pltpu.SemaphoreType.DMA((2,)), pltpu.SemaphoreType.DMA((5,)),
            pltpu.SemaphoreType.DMA((5, GROUPS)), pltpu.SemaphoreType.DMA((6,)),
            pltpu.SemaphoreType.DMA((6,)), pltpu.SemaphoreType.DMA((4, SETS)),
            pltpu.SemaphoreType.DMA((4, SETS)),
        ],
        compiler_params=pltpu.CompilerParams(
            collective_id=0, has_side_effects=True, vmem_limit_bytes=62 << 20
        ),
        cost_estimate=pl.CostEstimate(
            flops=60_000_000_000, bytes_accessed=20 << 20, transcendentals=0
        ),
    )(jump_rhs, w_factor, s_factor, rigid_coarse_blocks, coarse_factor, slot, pair_counts, corner)


def solution(mesh):
    each = ("set", "sub")
    return jax.shard_map(
        body,
        mesh=mesh,
        in_specs=(
            P(None, each), P(each, None, None), P(each, None, None), P(each, None, None),
            P("set", None), P(each), P(each, None), P(each, None),
        ),
        out_specs=(P(None, each), P(None, each)),
        check_vma=False,
    )
```

```python
import jax
import jax.numpy as jnp
from jax import lax
from jax.experimental import pallas as pl
from jax.experimental.pallas import tpu as pltpu
from jax.sharding import PartitionSpec as P

f32 = jnp.float32
bf16 = jnp.bfloat16
MESH = pl.DeviceIdType.MESH
HI = lax.Precision.HIGHEST

L = 32
PEERS = 32
SETS = 4
CAP = 256
RD = 8192
SD = 16
RM = 512
NC = 8
NK = SD * NC
NCO = 512
QS = NCO // NK
GROUP = 8
GROUPS = PEERS // GROUP

NT = (((1,), (1,)), ((), ()))


def dot(a, b):
    return jnp.dot(a, b, preferred_element_type=f32)


def dot_nt(a, b):
    return lax.dot_general(a, b, NT, preferred_element_type=f32)


def at(i, n):
    return pl.ds(pl.multiple_of(i * n, n), n)


def loop(n, f):
    def step(i, carry):
        f(i)
        return carry

    lax.fori_loop(0, n, step, 0)


def split(x):
    high = x.astype(bf16)
    return high, (x - high.astype(f32)).astype(bf16)


def kernel(
    jump, w_hbm, s_hbm, blocks, factor, slot, counts, corner,
    mult, resid,
    W, V, B, BT, Xm, live, jr, f, p, d, kd, pk,
    send, recv, csend, crecv, cpad, crow, Cbd, Ce, OHT,
    gsend, grecv, hsend, hrecv, back, pks, psend, precv, qsend, qrecv, acc, acc0,
    sa, wsem, assem, arsem, ssem, rsem, qssem, qrsem,
):
    st = lax.axis_index("set")
    me = lax.axis_index("sub")
    mg = me // GROUP

    copy_v = pltpu.make_async_copy(s_hbm, V, wsem.at[0])
    copy_w = pltpu.make_async_copy(w_hbm, W, wsem.at[1])
    copy_v.start()
    copy_w.start()

    barrier = pltpu.get_barrier_semaphore()

    def greet(k):
        pl.semaphore_signal(
            barrier, inc=1, device_id=(st, lax.rem(me + 1 + k, PEERS)), device_id_type=MESH
        )

    def greet_set(k):
        pl.semaphore_signal(
            barrier, inc=1, device_id=(lax.rem(st + 1 + k, SETS), me), device_id_type=MESH
        )

    loop(PEERS - 1, greet)
    loop(SETS - 1, greet_set)

    def wrap(q):
        return jnp.where(q >= PEERS, q - PEERS, q)

    def others(f):
        for k in range(1, PEERS):
            f(wrap(me + k))

    def send_all(n, src, dst):
        others(
            lambda q: pltpu.make_async_remote_copy(
                src_ref=src(q), dst_ref=dst, send_sem=ssem.at[n], recv_sem=rsem.at[n],
                device_id=(st, q), device_id_type=MESH,
            ).start()
        )

    def wait_all(n, dst):
        copy = pltpu.make_async_remote_copy(
            src_ref=dst, dst_ref=dst, send_sem=ssem.at[n], recv_sem=rsem.at[n],
            device_id=(st, wrap(me + 1)), device_id_type=MESH,
        )
        copy.wait_recv()
        copy.wait_send()

    def block_copy(e, src, dst, g, q):
        return pltpu.make_async_remote_copy(
            src_ref=src, dst_ref=dst, send_sem=assem.at[e], recv_sem=arsem.at[e, g],
            device_id=(st, q), device_id_type=MESH,
        )

    def send_group(e, g):
        for k in range(GROUP):
            r = lax.rem(me, GROUP) + k
            q = g * GROUP + jnp.where(r >= GROUP, r - GROUP, r)

            @pl.when(q != me)
            def _():
                block_copy(e, send.at[q], recv.at[e % 3, me], mg, q).start()

    def wait_group(e, g, n):
        some = recv.at[e % 3, pl.ds(g * GROUP, n)]
        block_copy(e, some, some, g, wrap(me + 1)).wait_recv()

    def plane(i):
        return jnp.where(i == 0, 2, jnp.where(i == 3, 0, 2 * i - 1))

    def swap_pairs(x):
        lane = lax.broadcasted_iota(jnp.int32, x.shape, 1)
        n = x.shape[1]
        return jnp.where(lane % 2 == 0, pltpu.roll(x, n - 1, 1), pltpu.roll(x, 1, 1))

    def slots_and_send(e, x, early=None):
        def one(i):
            g = lax.rem(mg + plane(i), GROUPS)
            for c in range(RD // CAP):
                cols = slice(c * CAP, (c + 1) * CAP)
                a = jnp.concatenate([sa[:, cols] - g * GROUP] * (L // 8), axis=0)
                v = x[:, cols]
                Xm[:, cols] = jnp.concatenate(
                    [jnp.where(a == k, v, 0.0).astype(bf16) for k in range(GROUP)], axis=0
                )
            send[pl.ds(g * GROUP, GROUP)] = dot(Xm[...], BT[...]).reshape(GROUP, L, CAP)
            if early is not None:
                pl.when(i == 0)(early)
            send_group(e, g)

        loop(GROUPS, one)
        recv[e % 3, me] = swap_pairs(send[me])

    def sent(e):
        most = send.at[pl.ds(0, PEERS - 1)]
        block_copy(e, most, most, mg, wrap(me + 1)).wait_send()

    def rows_of_group(g, blocks16, out, first):
        for c in range(RD // CAP):
            cols = slice(c * CAP, (c + 1) * CAP)
            a = jnp.concatenate([sa[:, cols] - g * GROUP] * (L // 8), axis=0)
            u = dot(blocks16, B[:, cols])
            res = out[:, cols]
            for k in range(GROUP):
                res = jnp.where(a == k, u[k * L : (k + 1) * L], res)
            out[:, cols] = res

    def receive_rows(e, out, change=None):
        out[...] = jnp.zeros_like(out)

        def one(i):
            g = lax.rem(mg + GROUPS - plane(i), GROUPS)
            pl.when(i < GROUPS - 1)(lambda: wait_group(e, g, GROUP))
            pl.when(i == GROUPS - 1)(lambda: wait_group(e, g, GROUP - 1))
            blk = recv[e % 3, pl.ds(g * GROUP, GROUP)].reshape(GROUP * L, CAP)
            if change is not None:
                blk = change(blk, g)
            rows_of_group(g, blk.astype(bf16), out, False)

        loop(GROUPS, one)
        most = send.at[pl.ds(0, PEERS - 1)]
        block_copy(e, most, most, mg, wrap(me + 1)).wait_send()

    def rows_again(e, out):
        out[...] = jnp.zeros_like(out)

        def one(g):
            blk = recv[e % 3, pl.ds(g * GROUP, GROUP)].reshape(GROUP * L, CAP)
            rows_of_group(g, blk.astype(bf16), out, False)

        loop(GROUPS, one)

    def gram(F):
        def one(i):
            for k in range(4):
                m = F[i * 4 + k]
                F[i * 4 + k] = dot_nt(m, m).astype(bf16)

        loop(SD // 4, one)

    def apply(x, F, scale):
        acc[...] = jnp.zeros_like(acc)

        def one(i):
            for k in range(4):
                s = i * 4 + k
                cols = at(s, RM)
                v = x[:, cols] * scale
                out = dot(v.astype(bf16), F[s])
                f[:, cols] = out
                prod = v * out
                acc[...] += sum(prod[:, n * 128 : (n + 1) * 128] for n in range(RM // 128))

        loop(SD // 4, one)

    def lanes_to_row(x):
        x = jnp.concatenate([x, jnp.zeros((128 - L, 128), f32)], axis=0)
        return jnp.sum(x.T, axis=0, keepdims=True)

    def row_to_column(x):
        return jnp.broadcast_to(x, (128, 128)).T[0:L]

    def sum_start():
        psend[0] = lanes_to_row(acc[...])
        precv[me] = psend[0]
        send_all(5, lambda q: psend.at[0], precv.at[me])

    def sum_middle():
        wait_all(5, precv.at[pl.ds(0, PEERS - 1)])
        sum_out(1, jnp.sum(precv[...], axis=0))

    def across(e, q):
        return pltpu.make_async_remote_copy(
            src_ref=qsend.at[e], dst_ref=qrecv.at[e, st], send_sem=qssem.at[e, q],
            recv_sem=qrsem.at[e, st], device_id=(q, me), device_id_type=MESH,
        )

    def across_arrival(e, q):
        return pltpu.make_async_remote_copy(
            src_ref=qsend.at[e], dst_ref=qrecv.at[e, q], send_sem=qssem.at[e, q],
            recv_sem=qrsem.at[e, q], device_id=(q, me), device_id_type=MESH,
        )

    def other_sets(f):
        loop(SETS - 1, lambda k: f(lax.rem(st + 1 + k, SETS)))

    def sum_out(e, total):
        total = jnp.concatenate([total, jnp.zeros((8 - total.shape[0], 128), f32)], axis=0)
        qsend[e] = total
        qrecv[e, st] = total
        other_sets(lambda q: across(e, q).start())

    def sum_end(e, n):
        other_sets(lambda q: across_arrival(e, q).wait_recv())
        other_sets(lambda q: across(e, q).wait_send())
        total = jnp.sum(qrecv[e], axis=0)
        return [row_to_column(total[r : r + 1]) for r in range(n)]

    def coarse_start(e):
        g = dot_nt(d[...].astype(bf16), Cbd[...])
        unknown = lax.broadcasted_iota(jnp.int32, (NK, NK), 0)
        hits = jnp.concatenate(
            [jnp.where((unknown + q * NK).astype(f32) == corner[0:1], 1.0, 0.0).astype(bf16)
             for q in range(QS)], axis=1
        )

        def spread(x):
            zero = jnp.zeros((L, NK), bf16)
            return jnp.concatenate(
                [jnp.concatenate([x if r == q else zero for r in range(QS)], axis=1)
                 for q in range(QS)], axis=0
            )

        high, low = split(g)
        x = dot_nt(hits, spread(high)) + dot_nt(hits, spread(low))
        for j in range(PEERS):
            gsend[e, j] = x[j * QS : (j + 1) * QS]
        grecv[e, me] = gsend[e, me]
        send_all(1 + e, lambda q: gsend.at[e, q], grecv.at[e, me])

    def coarse_sum(e):
        wait_all(1 + e, grecv.at[e, pl.ds(0, PEERS - 1)])
        hsend[e, 0:QS] = jnp.sum(grecv[e], axis=0)
        hsend[e, QS : QS + 1] = lanes_to_row(acc[...])
        hsend[e, QS + 1 : QS + 2] = lanes_to_row(acc0[...])
        hrecv[e, me] = hsend[e]
        send_all(3 + e, lambda q: hsend.at[e], hrecv.at[e, me])

    def coarse_solve(e):
        wait_all(3 + e, hrecv.at[e, pl.ds(0, PEERS - 1)])
        x = jnp.concatenate([hrecv[e, j, 0:QS] for j in range(PEERS)], axis=0).T
        sums = jnp.sum(hrecv[e, :, QS : QS + 2], axis=0)
        coarse_in = jnp.concatenate([x[q * L : (q + 1) * L] for q in range(QS)], axis=1)
        middle = jnp.dot(coarse_in, factor[...], precision=HI, preferred_element_type=f32)
        sol = lax.dot_general(
            middle, factor[...], NT, precision=HI, preferred_element_type=f32
        )
        both = dot(jnp.concatenate(split(sol), axis=0), OHT[...])
        back[...] = both[:L] + both[L:]
        kd[...] = dot(back[:, at(me, NK)].astype(bf16), Cbd[...])
        square = middle * middle
        square = lanes_to_row(sum(square[:, n * 128 : (n + 1) * 128] for n in range(NCO // 128)))
        sum_out(2 * e, jnp.concatenate([sums[0:1] + square, sums[1:2]], axis=0))

    def partners_coarse():
        def one(j):
            for k in range(4):
                q = j * 4 + k
                pks[at(q, L), :] = dot(back[:, at(q, NK)].astype(bf16), Ce[q])

        loop(PEERS // 4, one)

    def onehot(c):
        cols = at(c, CAP)
        hit = lax.broadcasted_iota(jnp.int32, (CAP, CAP), 0) == slot[0:1, cols] % CAP
        m = jnp.where(hit, 1.0, 0.0)
        B[:, cols] = m.astype(bf16)
        BT[cols, :] = m.T.astype(bf16)

    loop(RD // CAP, onehot)

    def live_rows(c):
        cols = at(c, RM)
        s = slot[0:1, cols]
        a = s // CAP
        sa[:, cols] = jnp.broadcast_to(a, (8, RM))
        n = jnp.zeros_like(s)
        for k in range(PEERS):
            n = jnp.where(a == k, counts[0, k], n)
        on = jnp.where(s % CAP < n, 1.0, 0.0)
        live[:, cols] = jnp.broadcast_to(on, (8, RM))
        resid[:, cols] = on * jump[:, cols]

    loop(RD // RM, live_rows)

    cpad[...] = jnp.zeros_like(cpad)
    for s in range(SD):
        for k in range(6):
            cpad[s, k : k + 1, :] = blocks[k, s : s + 1, :]
    Cbd[...] = jnp.zeros_like(Cbd)
    zero = jnp.zeros((NC, RM), f32)
    row = lax.broadcasted_iota(jnp.int32, (NC, RM), 0)
    for s in range(SD):
        crow[:, s * RM : (s + 1) * RM] = jnp.where(row == 6, float(s), cpad[s])
    for q in range(SD // 2):
        top = jnp.concatenate([cpad[2 * q], zero], axis=1)
        low = jnp.concatenate([zero, cpad[2 * q + 1]], axis=1)
        Cbd[2 * q * NC : (2 * q + 2) * NC, 2 * q * RM : (2 * q + 2) * RM] = jnp.concatenate(
            [top, low], axis=0
        ).astype(bf16)

    pl.semaphore_wait(barrier, PEERS - 1 + SETS - 1)

    slots_and_send(0, resid)

    def mask_modes(c):
        cols = at(c, CAP)
        a = sa[:, cols]
        v = crow[:, cols]
        Xm[:, cols] = jnp.concatenate(
            [jnp.where(a == k, v, 0.0) for k in range(PEERS)], axis=0
        ).astype(bf16)

    loop(RD // CAP, mask_modes)
    csend[...] = dot(Xm[...], BT[...]).reshape(PEERS, NC, CAP)
    csend[:, 7:8, 0:NK] = jnp.broadcast_to(corner[0:1].reshape(1, 1, NK), (PEERS, 1, NK))
    crecv[me] = swap_pairs(csend[me])
    crecv[me, 7:8, 0:NK] = corner[0:1]

    copy_v.wait()
    gram(V)
    receive_rows(0, p)
    send_all(0, lambda q: csend.at[q], crecv.at[me])

    def first(c):
        cols = at(c, RM)
        jr[:, cols] = resid[:, cols] + live[0:1, cols] * p[:, cols]

    loop(RD // RM, first)

    apply(jr, V, 1.0)
    acc0[...] = acc[...]
    slots_and_send(1, f)

    wait_all(0, crecv.at[pl.ds(0, PEERS - 1)])

    def expand(j):
        blk = crecv[j]
        sub = jnp.broadcast_to(blk[6:7], (NC, CAP))
        for q in range(SD // 2):
            Ce[j, 2 * q * NC : (2 * q + 2) * NC, :] = jnp.concatenate(
                [jnp.where(sub == float(2 * q), blk, 0.0),
                 jnp.where(sub == float(2 * q + 1), blk, 0.0)], axis=0
            ).astype(bf16)
        unknown = lax.broadcasted_iota(jnp.int32, (NCO, NK), 0).astype(f32)
        OHT[:, at(j, NK)] = jnp.where(unknown == blk[7:8, 0:NK], 1.0, 0.0).astype(bf16)

    loop(PEERS, expand)
    copy_w.wait()
    gram(W)

    receive_rows(1, p)

    def first_direction(c):
        cols = at(c, RM)
        d[:, cols] = live[0:1, cols] * (f[:, cols] + p[:, cols])

    loop(RD // RM, first_direction)

    coarse_start(0)
    apply(d, W, 2.0)
    slots_and_send(2, f, lambda: coarse_sum(0))
    coarse_solve(0)
    partners_coarse()
    receive_rows(2, p, lambda blk, g: 2.0 * blk + pks[at(g, GROUP * L), :])
    curvature, energy = sum_end(0, 2)
    alpha = energy / curvature

    def update(c):
        cols = at(c, RM)
        on = live[0:1, cols]
        al = alpha[:, 0:1]
        part = f[:, cols] + kd[:, cols]
        mult[:, cols] = al * d[:, cols]
        resid[:, cols] -= al * (on * part)
        jr[:, cols] -= al * (on * (part + f[:, cols] + p[:, cols]))

    loop(RD // RM, update)

    apply(jr, V, 1.0)
    sum_start()
    slots_and_send(3, f)
    sum_middle()
    rows_again(2, pk)
    receive_rows(3, p)
    (new,) = sum_end(1, 1)
    beta = new / energy

    def next_direction(c):
        cols = at(c, RM)
        on = live[0:1, cols]
        resid[:, cols] -= alpha[:, 0:1] * (on * pk[:, cols])
        d[:, cols] = on * (f[:, cols] + p[:, cols]) + beta[:, 0:1] * d[:, cols]

    loop(RD // RM, next_direction)

    coarse_start(1)
    apply(d, W, 2.0)
    slots_and_send(4, f, lambda: coarse_sum(1))
    coarse_solve(1)
    receive_rows(4, p)
    (curvature,) = sum_end(2, 1)
    alpha2 = new / curvature

    def last(c):
        cols = at(c, RM)
        al = alpha2[:, 0:1]
        mult[:, cols] += al * d[:, cols]
        resid[:, cols] -= al * (live[0:1, cols] * (f[:, cols] + p[:, cols] + kd[:, cols]))

    loop(RD // RM, last)


def hand_on(a, b, a_out, b_out, buf, sem_in, sem_out):
    pairs = [
        (n * (L // 8) + k, x.at[8 * k : 8 * k + 8], y.at[8 * k : 8 * k + 8])
        for n, (x, y) in enumerate(((a, a_out), (b, b_out)))
        for k in range(L // 8)
    ]
    first = [pltpu.make_async_copy(x, buf.at[i], sem_in.at[i]) for i, x, _ in pairs]
    second = [pltpu.make_async_copy(buf.at[i], y, sem_out.at[i]) for i, _, y in pairs]
    for copy in first:
        copy.start()
    for one, two in zip(first, second):
        one.wait()
        two.start()
    for copy in second:
        copy.wait()


def body(
    jump_rhs, w_factor, s_factor, rigid_coarse_blocks, coarse_factor, slot_of_row, pair_counts,
    corner_map,
):
    slot = slot_of_row.reshape(1, RD)
    corner = jnp.pad(corner_map.astype(f32), ((0, 0), (0, 2)), constant_values=-1.0)
    corner = corner.reshape(1, NK)
    rigid_coarse_blocks = jnp.transpose(rigid_coarse_blocks, (1, 0, 2))
    vm = pl.BlockSpec(memory_space=pltpu.VMEM)
    hbm = pl.BlockSpec(memory_space=pl.ANY)
    sm = pl.BlockSpec(memory_space=pltpu.SMEM)
    V = pltpu.VMEM
    vec = V((L, RD), f32)
    results = pl.pallas_call(
        kernel,
        out_shape=(jax.ShapeDtypeStruct((L, RD), f32),) * 2,
        in_specs=[vm, hbm, hbm, vm, vm, vm, sm, vm],
        out_specs=[vm, vm],
        scratch_shapes=[
            V((SD, RM, RM), bf16), V((SD, RM, RM), bf16), V((CAP, RD), bf16), V((RD, CAP), bf16),
            V((GROUP * L, RD), bf16), V((8, RD), f32), vec, vec, vec, vec, vec, vec,
            V((PEERS, L, CAP), f32), V((3, PEERS, L, CAP), f32), V((PEERS, NC, CAP), f32),
            V((PEERS, NC, CAP), f32), V((SD, NC, RM), f32), V((NC, RD), f32), V((NK, RD), bf16),
            V((PEERS, NK, CAP), bf16), V((NCO, PEERS * NK), bf16),
            V((2, PEERS, QS, NK), f32), V((2, PEERS, QS, NK), f32), V((2, 8, NK), f32),
            V((2, PEERS, 8, NK), f32),
            V((L, PEERS * NK), f32), V((PEERS * L, CAP), f32),
            V((1, 1, 128), f32), V((PEERS, 1, 128), f32), V((3, 8, 128), f32),
            V((3, SETS, 8, 128), f32), V((L, 128), f32), V((L, 128), f32), V((8, RD), jnp.int32),
            pltpu.SemaphoreType.DMA((2,)), pltpu.SemaphoreType.DMA((5,)),
            pltpu.SemaphoreType.DMA((5, GROUPS)), pltpu.SemaphoreType.DMA((6,)),
            pltpu.SemaphoreType.DMA((6,)), pltpu.SemaphoreType.DMA((4, SETS)),
            pltpu.SemaphoreType.DMA((4, SETS)),
        ],
        compiler_params=pltpu.CompilerParams(
            collective_id=0, has_side_effects=True, vmem_limit_bytes=62 << 20
        ),
        cost_estimate=pl.CostEstimate(
            flops=60_000_000_000, bytes_accessed=20 << 20, transcendentals=0
        ),
    )(jump_rhs, w_factor, s_factor, rigid_coarse_blocks, coarse_factor, slot, pair_counts, corner)
    return pl.pallas_call(
        hand_on,
        out_shape=(jax.ShapeDtypeStruct((L, RD), f32),) * 2,
        in_specs=[hbm, hbm],
        out_specs=[hbm, hbm],
        scratch_shapes=[
            V((L // 4, 8, RD), f32), pltpu.SemaphoreType.DMA((L // 4,)),
            pltpu.SemaphoreType.DMA((L // 4,)),
        ],
    )(*results)


def solution(mesh):
    each = ("set", "sub")
    return jax.shard_map(
        body,
        mesh=mesh,
        in_specs=(
            P(None, each), P(each, None, None), P(each, None, None), P(each, None, None),
            P("set", None), P(each), P(each, None), P(each, None),
        ),
        out_specs=(P(None, each), P(None, each)),
        check_vma=False,
    )
```

```python
import jax
import jax.numpy as jnp
from jax import lax
from jax.experimental import pallas as pl
from jax.experimental.pallas import tpu as pltpu
from jax.sharding import PartitionSpec as P

f32 = jnp.float32
bf16 = jnp.bfloat16
MESH = pl.DeviceIdType.MESH
HI = lax.Precision.HIGHEST

L = 32
PEERS = 32
SETS = 4
CAP = 256
RD = 8192
SD = 16
RM = 512
NC = 8
NK = SD * NC
NCO = 512
QS = NCO // NK
GROUP = 8
GROUPS = PEERS // GROUP

NT = (((1,), (1,)), ((), ()))


def dot(a, b):
    return jnp.dot(a, b, preferred_element_type=f32)


def dot_nt(a, b):
    return lax.dot_general(a, b, NT, preferred_element_type=f32)


def at(i, n):
    return pl.ds(pl.multiple_of(i * n, n), n)


def loop(n, f):
    def step(i, carry):
        f(i)
        return carry

    lax.fori_loop(0, n, step, 0)


def split(x):
    high = x.astype(bf16)
    return high, (x - high.astype(f32)).astype(bf16)


def kernel(
    jump, w_hbm, s_hbm, blocks, factor, slot, counts, corners,
    mult, resid,
    W, V, B, BT, Xm, live, jr, f, p, d, kd, pk,
    send, recv, csend, crecv, cpad, crow, Cbd, Ce, OHT,
    gsend, grecv, hsend, hrecv, back, pks, psend, precv, qsend, qrecv, acc, acc0,
    sa, corner, wsem, assem, arsem, ssem, rsem, qssem, qrsem,
):
    st = lax.axis_index("set")
    me = lax.axis_index("sub")
    mg = me // GROUP

    copy_v = pltpu.make_async_copy(s_hbm, V, wsem.at[0])
    copy_w = pltpu.make_async_copy(w_hbm, W, wsem.at[1])
    copy_v.start()
    copy_w.start()

    barrier = pltpu.get_barrier_semaphore()

    def greet(k):
        pl.semaphore_signal(
            barrier, inc=1, device_id=(st, lax.rem(me + 1 + k, PEERS)), device_id_type=MESH
        )

    def greet_set(k):
        pl.semaphore_signal(
            barrier, inc=1, device_id=(lax.rem(st + 1 + k, SETS), me), device_id_type=MESH
        )

    loop(PEERS - 1, greet)
    loop(SETS - 1, greet_set)

    def wrap(q):
        return jnp.where(q >= PEERS, q - PEERS, q)

    def others(f):
        for k in range(1, PEERS):
            f(wrap(me + k))

    def send_all(n, src, dst):
        others(
            lambda q: pltpu.make_async_remote_copy(
                src_ref=src(q), dst_ref=dst, send_sem=ssem.at[n], recv_sem=rsem.at[n],
                device_id=(st, q), device_id_type=MESH,
            ).start()
        )

    def wait_all(n, dst):
        copy = pltpu.make_async_remote_copy(
            src_ref=dst, dst_ref=dst, send_sem=ssem.at[n], recv_sem=rsem.at[n],
            device_id=(st, wrap(me + 1)), device_id_type=MESH,
        )
        copy.wait_recv()
        copy.wait_send()

    def block_copy(e, src, dst, g, q):
        return pltpu.make_async_remote_copy(
            src_ref=src, dst_ref=dst, send_sem=assem.at[e], recv_sem=arsem.at[e, g],
            device_id=(st, q), device_id_type=MESH,
        )

    def send_group(e, g):
        for k in range(GROUP):
            r = lax.rem(me, GROUP) + k
            q = g * GROUP + jnp.where(r >= GROUP, r - GROUP, r)

            @pl.when(q != me)
            def _():
                block_copy(e, send.at[q], recv.at[e % 3, me], mg, q).start()

    def wait_group(e, g, n):
        some = recv.at[e % 3, pl.ds(g * GROUP, n)]
        block_copy(e, some, some, g, wrap(me + 1)).wait_recv()

    def plane(i):
        return jnp.where(i == 0, 2, jnp.where(i == 3, 0, 2 * i - 1))

    def swap_pairs(x):
        lane = lax.broadcasted_iota(jnp.int32, x.shape, 1)
        n = x.shape[1]
        return jnp.where(lane % 2 == 0, pltpu.roll(x, n - 1, 1), pltpu.roll(x, 1, 1))

    def slots_and_send(e, x, early=None):
        def one(i):
            g = lax.rem(mg + plane(i), GROUPS)
            for c in range(RD // CAP):
                cols = slice(c * CAP, (c + 1) * CAP)
                a = jnp.concatenate([sa[:, cols] - g * GROUP] * (L // 8), axis=0)
                v = x[:, cols]
                Xm[:, cols] = jnp.concatenate(
                    [jnp.where(a == k, v, 0.0).astype(bf16) for k in range(GROUP)], axis=0
                )
            send[pl.ds(g * GROUP, GROUP)] = dot(Xm[...], BT[...]).reshape(GROUP, L, CAP)
            if early is not None:
                pl.when(i == 0)(early)
            send_group(e, g)

        loop(GROUPS, one)
        recv[e % 3, me] = swap_pairs(send[me])

    def sent(e):
        most = send.at[pl.ds(0, PEERS - 1)]
        block_copy(e, most, most, mg, wrap(me + 1)).wait_send()

    def rows_of_group(g, blocks16, out, first):
        for c in range(RD // CAP):
            cols = slice(c * CAP, (c + 1) * CAP)
            a = jnp.concatenate([sa[:, cols] - g * GROUP] * (L // 8), axis=0)
            u = dot(blocks16, B[:, cols])
            res = out[:, cols]
            for k in range(GROUP):
                res = jnp.where(a == k, u[k * L : (k + 1) * L], res)
            out[:, cols] = res

    def receive_rows(e, out, change=None):
        out[...] = jnp.zeros_like(out)

        def one(i):
            g = lax.rem(mg + GROUPS - plane(i), GROUPS)
            pl.when(i < GROUPS - 1)(lambda: wait_group(e, g, GROUP))
            pl.when(i == GROUPS - 1)(lambda: wait_group(e, g, GROUP - 1))
            blk = recv[e % 3, pl.ds(g * GROUP, GROUP)].reshape(GROUP * L, CAP)
            if change is not None:
                blk = change(blk, g)
            rows_of_group(g, blk.astype(bf16), out, False)

        loop(GROUPS, one)
        most = send.at[pl.ds(0, PEERS - 1)]
        block_copy(e, most, most, mg, wrap(me + 1)).wait_send()

    def rows_again(e, out):
        out[...] = jnp.zeros_like(out)

        def one(g):
            blk = recv[e % 3, pl.ds(g * GROUP, GROUP)].reshape(GROUP * L, CAP)
            rows_of_group(g, blk.astype(bf16), out, False)

        loop(GROUPS, one)

    def gram(F):
        def one(i):
            for k in range(4):
                m = F[i * 4 + k]
                F[i * 4 + k] = dot_nt(m, m).astype(bf16)

        loop(SD // 4, one)

    def apply(x, F, scale):
        acc[...] = jnp.zeros_like(acc)

        def one(i):
            for k in range(4):
                s = i * 4 + k
                cols = at(s, RM)
                v = x[:, cols] * scale
                out = dot(v.astype(bf16), F[s])
                f[:, cols] = out
                prod = v * out
                acc[...] += sum(prod[:, n * 128 : (n + 1) * 128] for n in range(RM // 128))

        loop(SD // 4, one)

    def lanes_to_row(x):
        x = jnp.concatenate([x, jnp.zeros((128 - L, 128), f32)], axis=0)
        return jnp.sum(x.T, axis=0, keepdims=True)

    def row_to_column(x):
        return jnp.broadcast_to(x, (128, 128)).T[0:L]

    def sum_start():
        psend[0] = lanes_to_row(acc[...])
        precv[me] = psend[0]
        send_all(5, lambda q: psend.at[0], precv.at[me])

    def sum_middle():
        wait_all(5, precv.at[pl.ds(0, PEERS - 1)])
        sum_out(1, jnp.sum(precv[...], axis=0))

    def across(e, q):
        return pltpu.make_async_remote_copy(
            src_ref=qsend.at[e], dst_ref=qrecv.at[e, st], send_sem=qssem.at[e, q],
            recv_sem=qrsem.at[e, st], device_id=(q, me), device_id_type=MESH,
        )

    def across_arrival(e, q):
        return pltpu.make_async_remote_copy(
            src_ref=qsend.at[e], dst_ref=qrecv.at[e, q], send_sem=qssem.at[e, q],
            recv_sem=qrsem.at[e, q], device_id=(q, me), device_id_type=MESH,
        )

    def other_sets(f):
        loop(SETS - 1, lambda k: f(lax.rem(st + 1 + k, SETS)))

    def sum_out(e, total):
        total = jnp.concatenate([total, jnp.zeros((8 - total.shape[0], 128), f32)], axis=0)
        qsend[e] = total
        qrecv[e, st] = total
        other_sets(lambda q: across(e, q).start())

    def sum_end(e, n):
        other_sets(lambda q: across_arrival(e, q).wait_recv())
        other_sets(lambda q: across(e, q).wait_send())
        total = jnp.sum(qrecv[e], axis=0)
        return [row_to_column(total[r : r + 1]) for r in range(n)]

    def coarse_start(e):
        g = dot_nt(d[...].astype(bf16), Cbd[...])
        unknown = lax.broadcasted_iota(jnp.int32, (NK, NK), 0)
        hits = jnp.concatenate(
            [jnp.where((unknown + q * NK).astype(f32) == corner[0:1], 1.0, 0.0).astype(bf16)
             for q in range(QS)], axis=1
        )

        def spread(x):
            zero = jnp.zeros((L, NK), bf16)
            return jnp.concatenate(
                [jnp.concatenate([x if r == q else zero for r in range(QS)], axis=1)
                 for q in range(QS)], axis=0
            )

        high, low = split(g)
        x = dot_nt(hits, spread(high)) + dot_nt(hits, spread(low))
        for j in range(PEERS):
            gsend[e, j] = x[j * QS : (j + 1) * QS]
        grecv[e, me] = gsend[e, me]
        send_all(1 + e, lambda q: gsend.at[e, q], grecv.at[e, me])

    def coarse_sum(e):
        wait_all(1 + e, grecv.at[e, pl.ds(0, PEERS - 1)])
        hsend[e, 0:QS] = jnp.sum(grecv[e], axis=0)
        hsend[e, QS : QS + 1] = lanes_to_row(acc[...])
        hsend[e, QS + 1 : QS + 2] = lanes_to_row(acc0[...])
        hrecv[e, me] = hsend[e]
        send_all(3 + e, lambda q: hsend.at[e], hrecv.at[e, me])

    def coarse_solve(e):
        wait_all(3 + e, hrecv.at[e, pl.ds(0, PEERS - 1)])
        x = jnp.concatenate([hrecv[e, j, 0:QS] for j in range(PEERS)], axis=0).T
        sums = jnp.sum(hrecv[e, :, QS : QS + 2], axis=0)
        coarse_in = jnp.concatenate([x[q * L : (q + 1) * L] for q in range(QS)], axis=1)
        middle = jnp.dot(coarse_in, factor[...], precision=HI, preferred_element_type=f32)
        sol = lax.dot_general(
            middle, factor[...], NT, precision=HI, preferred_element_type=f32
        )
        both = dot(jnp.concatenate(split(sol), axis=0), OHT[...])
        back[...] = both[:L] + both[L:]
        kd[...] = dot(back[:, at(me, NK)].astype(bf16), Cbd[...])
        square = middle * middle
        square = lanes_to_row(sum(square[:, n * 128 : (n + 1) * 128] for n in range(NCO // 128)))
        sum_out(2 * e, jnp.concatenate([sums[0:1] + square, sums[1:2]], axis=0))

    def partners_coarse():
        def one(j):
            for k in range(4):
                q = j * 4 + k
                pks[at(q, L), :] = dot(back[:, at(q, NK)].astype(bf16), Ce[q])

        loop(PEERS // 4, one)

    def onehot(c):
        cols = at(c, CAP)
        hit = lax.broadcasted_iota(jnp.int32, (CAP, CAP), 0) == slot[0:1, cols] % CAP
        m = jnp.where(hit, 1.0, 0.0)
        B[:, cols] = m.astype(bf16)
        BT[cols, :] = m.T.astype(bf16)

    loop(RD // CAP, onehot)

    def live_rows(c):
        cols = at(c, RM)
        s = slot[0:1, cols]
        a = s // CAP
        sa[:, cols] = jnp.broadcast_to(a, (8, RM))
        n = jnp.zeros_like(s)
        for k in range(PEERS):
            n = jnp.where(a == k, counts[0, k], n)
        on = jnp.where(s % CAP < n, 1.0, 0.0)
        live[:, cols] = jnp.broadcast_to(on, (8, RM))
        resid[:, cols] = on * jump[:, cols]

    loop(RD // RM, live_rows)

    place = lax.broadcasted_iota(jnp.int32, (1, NK), 1)
    unknown = jnp.full((1, NK), -1, jnp.int32)
    for s in range(SD):
        for k in range(6):
            unknown = jnp.where(place == s * NC + k, corners[k, s], unknown)
    corner[...] = unknown.astype(f32)

    cpad[...] = jnp.zeros_like(cpad)
    for s in range(SD):
        for k in range(6):
            cpad[s, k : k + 1, :] = blocks[k, s : s + 1, :]
    Cbd[...] = jnp.zeros_like(Cbd)
    zero = jnp.zeros((NC, RM), f32)
    row = lax.broadcasted_iota(jnp.int32, (NC, RM), 0)
    for s in range(SD):
        crow[:, s * RM : (s + 1) * RM] = jnp.where(row == 6, float(s), cpad[s])
    for q in range(SD // 2):
        top = jnp.concatenate([cpad[2 * q], zero], axis=1)
        low = jnp.concatenate([zero, cpad[2 * q + 1]], axis=1)
        Cbd[2 * q * NC : (2 * q + 2) * NC, 2 * q * RM : (2 * q + 2) * RM] = jnp.concatenate(
            [top, low], axis=0
        ).astype(bf16)

    pl.semaphore_wait(barrier, PEERS - 1 + SETS - 1)

    slots_and_send(0, resid)

    def mask_modes(c):
        cols = at(c, CAP)
        a = sa[:, cols]
        v = crow[:, cols]
        Xm[:, cols] = jnp.concatenate(
            [jnp.where(a == k, v, 0.0) for k in range(PEERS)], axis=0
        ).astype(bf16)

    loop(RD // CAP, mask_modes)
    csend[...] = dot(Xm[...], BT[...]).reshape(PEERS, NC, CAP)
    csend[:, 7:8, 0:NK] = jnp.broadcast_to(corner[0:1].reshape(1, 1, NK), (PEERS, 1, NK))
    crecv[me] = swap_pairs(csend[me])
    crecv[me, 7:8, 0:NK] = corner[0:1]

    copy_v.wait()
    gram(V)
    receive_rows(0, p)
    send_all(0, lambda q: csend.at[q], crecv.at[me])

    def first(c):
        cols = at(c, RM)
        jr[:, cols] = resid[:, cols] + live[0:1, cols] * p[:, cols]

    loop(RD // RM, first)

    apply(jr, V, 1.0)
    acc0[...] = acc[...]
    slots_and_send(1, f)

    wait_all(0, crecv.at[pl.ds(0, PEERS - 1)])

    def expand(j):
        blk = crecv[j]
        sub = jnp.broadcast_to(blk[6:7], (NC, CAP))
        for q in range(SD // 2):
            Ce[j, 2 * q * NC : (2 * q + 2) * NC, :] = jnp.concatenate(
                [jnp.where(sub == float(2 * q), blk, 0.0),
                 jnp.where(sub == float(2 * q + 1), blk, 0.0)], axis=0
            ).astype(bf16)
        unknown = lax.broadcasted_iota(jnp.int32, (NCO, NK), 0).astype(f32)
        OHT[:, at(j, NK)] = jnp.where(unknown == blk[7:8, 0:NK], 1.0, 0.0).astype(bf16)

    loop(PEERS, expand)
    copy_w.wait()
    gram(W)

    receive_rows(1, p)

    def first_direction(c):
        cols = at(c, RM)
        d[:, cols] = live[0:1, cols] * (f[:, cols] + p[:, cols])

    loop(RD // RM, first_direction)

    coarse_start(0)
    apply(d, W, 2.0)
    slots_and_send(2, f, lambda: coarse_sum(0))
    coarse_solve(0)
    partners_coarse()
    receive_rows(2, p, lambda blk, g: 2.0 * blk + pks[at(g, GROUP * L), :])
    curvature, energy = sum_end(0, 2)
    alpha = energy / curvature

    def update(c):
        cols = at(c, RM)
        on = live[0:1, cols]
        al = alpha[:, 0:1]
        part = f[:, cols] + kd[:, cols]
        mult[:, cols] = al * d[:, cols]
        resid[:, cols] -= al * (on * part)
        jr[:, cols] -= al * (on * (part + f[:, cols] + p[:, cols]))

    loop(RD // RM, update)

    apply(jr, V, 1.0)
    sum_start()
    slots_and_send(3, f)
    sum_middle()
    rows_again(2, pk)
    receive_rows(3, p)
    (new,) = sum_end(1, 1)
    beta = new / energy

    def next_direction(c):
        cols = at(c, RM)
        on = live[0:1, cols]
        resid[:, cols] -= alpha[:, 0:1] * (on * pk[:, cols])
        d[:, cols] = on * (f[:, cols] + p[:, cols]) + beta[:, 0:1] * d[:, cols]

    loop(RD // RM, next_direction)

    coarse_start(1)
    apply(d, W, 2.0)
    slots_and_send(4, f, lambda: coarse_sum(1))
    coarse_solve(1)
    receive_rows(4, p)
    (curvature,) = sum_end(2, 1)
    alpha2 = new / curvature

    def last(c):
        cols = at(c, RM)
        al = alpha2[:, 0:1]
        mult[:, cols] += al * d[:, cols]
        resid[:, cols] -= al * (live[0:1, cols] * (f[:, cols] + p[:, cols] + kd[:, cols]))

    loop(RD // RM, last)


def hand_on(a, b, a_out, b_out, buf, sem_in, sem_out):
    pairs = [
        (n * (L // 8) + k, x.at[8 * k : 8 * k + 8], y.at[8 * k : 8 * k + 8])
        for n, (x, y) in enumerate(((a, a_out), (b, b_out)))
        for k in range(L // 8)
    ]
    first = [pltpu.make_async_copy(x, buf.at[i], sem_in.at[i]) for i, x, _ in pairs]
    second = [pltpu.make_async_copy(buf.at[i], y, sem_out.at[i]) for i, _, y in pairs]
    for copy in first:
        copy.start()
    for one, two in zip(first, second):
        one.wait()
        two.start()
    for copy in second:
        copy.wait()


def body(
    jump_rhs, w_factor, s_factor, rigid_coarse_blocks, coarse_factor, slot_of_row, pair_counts,
    corner_map,
):
    slot = slot_of_row.reshape(1, RD)
    corners = jnp.transpose(corner_map)
    rigid_coarse_blocks = jnp.transpose(rigid_coarse_blocks, (1, 0, 2))
    vm = pl.BlockSpec(memory_space=pltpu.VMEM)
    hbm = pl.BlockSpec(memory_space=pl.ANY)
    sm = pl.BlockSpec(memory_space=pltpu.SMEM)
    V = pltpu.VMEM
    vec = V((L, RD), f32)
    results = pl.pallas_call(
        kernel,
        out_shape=(jax.ShapeDtypeStruct((L, RD), f32),) * 2,
        in_specs=[vm, hbm, hbm, vm, vm, vm, sm, sm],
        out_specs=[vm, vm],
        scratch_shapes=[
            V((SD, RM, RM), bf16), V((SD, RM, RM), bf16), V((CAP, RD), bf16), V((RD, CAP), bf16),
            V((GROUP * L, RD), bf16), V((8, RD), f32), vec, vec, vec, vec, vec, vec,
            V((PEERS, L, CAP), f32), V((3, PEERS, L, CAP), f32), V((PEERS, NC, CAP), f32),
            V((PEERS, NC, CAP), f32), V((SD, NC, RM), f32), V((NC, RD), f32), V((NK, RD), bf16),
            V((PEERS, NK, CAP), bf16), V((NCO, PEERS * NK), bf16),
            V((2, PEERS, QS, NK), f32), V((2, PEERS, QS, NK), f32), V((2, 8, NK), f32),
            V((2, PEERS, 8, NK), f32),
            V((L, PEERS * NK), f32), V((PEERS * L, CAP), f32),
            V((1, 1, 128), f32), V((PEERS, 1, 128), f32), V((3, 8, 128), f32),
            V((3, SETS, 8, 128), f32), V((L, 128), f32), V((L, 128), f32), V((8, RD), jnp.int32), V((1, NK), f32),
            pltpu.SemaphoreType.DMA((2,)), pltpu.SemaphoreType.DMA((5,)),
            pltpu.SemaphoreType.DMA((5, GROUPS)), pltpu.SemaphoreType.DMA((6,)),
            pltpu.SemaphoreType.DMA((6,)), pltpu.SemaphoreType.DMA((4, SETS)),
            pltpu.SemaphoreType.DMA((4, SETS)),
        ],
        compiler_params=pltpu.CompilerParams(
            collective_id=0, has_side_effects=True, vmem_limit_bytes=62 << 20
        ),
        cost_estimate=pl.CostEstimate(
            flops=60_000_000_000, bytes_accessed=20 << 20, transcendentals=0
        ),
    )(jump_rhs, w_factor, s_factor, rigid_coarse_blocks, coarse_factor, slot, pair_counts, corners)
    return pl.pallas_call(
        hand_on,
        out_shape=(jax.ShapeDtypeStruct((L, RD), f32),) * 2,
        in_specs=[hbm, hbm],
        out_specs=[hbm, hbm],
        scratch_shapes=[
            V((L // 4, 8, RD), f32), pltpu.SemaphoreType.DMA((L // 4,)),
            pltpu.SemaphoreType.DMA((L // 4,)),
        ],
    )(*results)


def solution(mesh):
    each = ("set", "sub")
    return jax.shard_map(
        body,
        mesh=mesh,
        in_specs=(
            P(None, each), P(each, None, None), P(each, None, None), P(each, None, None),
            P("set", None), P(each), P(each, None), P(each, None),
        ),
        out_specs=(P(None, each), P(None, each)),
        check_vma=False,
    )
```
